1024 devices in a mesh: row: 8 (over z), col: 128 (over y, x, core).
Axes of the slice: x: 8, y: 8, z: 8, core: 2. Of those that a mesh axis runs over, the one named last changes fastest.
Arguments:
- coarse_scalar: float32 [512, 1024, 128], P('row', 'col'), may hold values from -6 to 6
- coarse_velocity: float32 [3, 512, 1024, 128], P(None, 'row', 'col'), may hold values from -0.5 to 0.5
- coarse_previous: float32 [3, 512, 1024, 128], P(None, 'row', 'col'), may hold values from -0.5 to 0.5
- fine_scalar: float32 [256, 1024, 128], P('row', 'col'), may hold values from -6 to 6
- fine_velocity: float32 [3, 256, 1024, 128], P(None, 'row', 'col'), may hold values from -0.5 to 0.5
- fine_previous: float32 [3, 256, 1024, 128], P(None, 'row', 'col'), may hold values from -0.5 to 0.5
- parent_shift: int32 [8, 128], P('row'), may hold values from -3 to 3, as said below
- offset_y: int32 [8, 128], P('row'), may hold values from 1 to 3
- offset_z: int32 [8, 128], P('row'), may hold values from 1 to 63
Outputs:
- coarse_result: float32 [512, 1024, 128], P('row', 'col')
- fine_result: float32 [256, 1024, 128], P('row', 'col')
The draws below stay inside these ranges and needn't reach their ends.
Inputs may be any that keep to these rules, and one draw needn't show every extreme that they name: `parent_shift`: in every aligned block of four columns of a row, every fine box's parent lies in the same block and never in its own column; one coarse box of each block is the parent of three fine boxes, another of one.
All inputs are finite; a program needn't handle non-finite values.
Results may differ from the reference program's by a relative error of at most 0.0003.
Values sent between devices are 32-bit elements; how exact they have to be, the bound alone decides.
A program may use at most 64 MiB of HBM per device.

```python
import jax
import jax.numpy as jnp
from jax import lax

CX = 64
CY = 8
CZ = 128
FX = 32
FY = 8
FZ = 128
BOX_ROWS = 8
BOX_COLS = 128
NX = 512
NY = 1024


def draw_parent_shift(key, part):
    key = jax.random.fold_in(key, 11)
    hub_key, partner_key = jax.random.split(key)
    blocks = BOX_COLS // 4
    hub_pos = jax.random.randint(hub_key, (BOX_ROWS, blocks), 0, 4)
    partner = jax.random.randint(partner_key, (BOX_ROWS, blocks), 0, 3)
    partner = jnp.where(partner >= hub_pos, partner + 1, partner)
    position = jnp.arange(4, dtype=jnp.int32)
    shifts = jnp.where(position == hub_pos[:, :, None], partner[:, :, None] - hub_pos[:, :, None], hub_pos[:, :, None] - position)
    return shifts.reshape(BOX_ROWS, BOX_COLS).astype(jnp.int32)


def plant(drawn, rng, least, top_value):
    spot = [jax.random.randint(jax.random.fold_in(rng, axis), (), 0, length) for axis, length in enumerate(drawn.shape)]
    widest = drawn.shape.index(max(drawn.shape))
    next_to = spot[:widest] + [(spot[widest] + 1) % drawn.shape[widest]] + spot[widest + 1:]
    return drawn.at[tuple(spot)].set(least).at[tuple(next_to)].set(top_value)


def level_of(rng, dims, cuts, least, largest):
    factor_of = 1.0
    for dim, parts in cuts:
        steps = jax.random.uniform(jax.random.fold_in(jax.random.fold_in(rng, 6), dim), (parts,), jnp.float32, least / len(cuts), largest / len(cuts))
        factor_of = factor_of * jnp.repeat(jnp.exp(steps), dims[dim] // parts).reshape((-1,) + (1,) * (len(dims) - 1 - dim))
    return factor_of


def centred(stream_key, shape, deviation, reach, shards=(), held_as=jnp.bfloat16):
    drawn = deviation * jax.random.normal(stream_key, shape, jnp.float32)
    if shards:
        drawn = drawn * level_of(stream_key, shape, shards, -0.22, 0.18)
    return jnp.clip(drawn, -reach, reach).astype(held_as)


def setup_inputs(seed: int = 0) -> dict:
    arg_keys = jax.random.split(jax.random.key(seed), 10)
    return {
        "coarse_scalar": centred(arg_keys[0], (NX, NY, CZ), 1.0, 6.0, ((0, 8), (1, 128)), jnp.float32),
        "coarse_velocity": jnp.clip(jax.random.uniform(arg_keys[1], (3, NX, NY, CZ), jnp.float32, -0.5, 0.5) * level_of(arg_keys[1], (3, NX, NY, CZ), ((1, 8), (2, 128)), -0.4, 0.0), -0.5, 0.5),
        "coarse_previous": jnp.clip(jax.random.uniform(arg_keys[2], (3, NX, NY, CZ), jnp.float32, -0.5, 0.5) * level_of(arg_keys[2], (3, NX, NY, CZ), ((1, 8), (2, 128)), -0.4, 0.0), -0.5, 0.5),
        "fine_scalar": centred(arg_keys[3], (FX * BOX_ROWS, FY * BOX_COLS, FZ), 1.0, 6.0, ((0, 8), (1, 128)), jnp.float32),
        "fine_velocity": jnp.clip(jax.random.uniform(arg_keys[4], (3, FX * BOX_ROWS, FY * BOX_COLS, FZ), jnp.float32, -0.5, 0.5) * level_of(arg_keys[4], (3, FX * BOX_ROWS, FY * BOX_COLS, FZ), ((1, 8), (2, 128)), -0.4, 0.0), -0.5, 0.5),
        "fine_previous": jnp.clip(jax.random.uniform(arg_keys[5], (3, FX * BOX_ROWS, FY * BOX_COLS, FZ), jnp.float32, -0.5, 0.5) * level_of(arg_keys[5], (3, FX * BOX_ROWS, FY * BOX_COLS, FZ), ((1, 8), (2, 128)), -0.4, 0.0), -0.5, 0.5),
        "parent_shift": draw_parent_shift(jax.random.fold_in(arg_keys[9], 71), 0),
        "offset_y": plant(jax.random.randint(arg_keys[7], (BOX_ROWS, BOX_COLS), 1, CY - FY // 2), jax.random.fold_in(arg_keys[7], 1), 1, (CY - FY // 2) - 1).astype(jnp.int32),
        "offset_z": plant(jax.random.randint(arg_keys[8], (BOX_ROWS, BOX_COLS), 1, CZ - FZ // 2), jax.random.fold_in(arg_keys[8], 1), 1, (CZ - FZ // 2) - 1).astype(jnp.int32),
    }


courant = 0.3


def as_index(values):
    return tuple(jnp.asarray(value).astype(jnp.int32) for value in values)


def minmod(left_diff, right_diff):
    return jnp.maximum(jnp.minimum(left_diff, right_diff), 0.0) + jnp.minimum(jnp.maximum(left_diff, right_diff), 0.0)


def take_range(values, direction, skip_low, skip_high):
    length = values.shape[direction]
    return lax.slice_in_dim(values, skip_low, length - skip_high, axis=direction)


def face_flux(scalar, velocity, direction):
    for across in range(3):
        if across != direction:
            scalar = take_range(scalar, across, 2, 2)
            velocity = take_range(velocity, across, 2, 2)
    step_below = take_range(scalar, direction, 1, 1) - take_range(scalar, direction, 0, 2)
    step_above = take_range(scalar, direction, 2, 0) - take_range(scalar, direction, 1, 1)
    slopes = minmod(step_below, step_above)
    face_speed = 0.5 * (take_range(velocity, direction, 1, 2) + take_range(velocity, direction, 2, 1))
    left_state = take_range(scalar, direction, 1, 2) + 0.5 * (1.0 - courant * face_speed) * take_range(slopes, direction, 0, 1)
    right_state = take_range(scalar, direction, 2, 1) - 0.5 * (1.0 + courant * face_speed) * take_range(slopes, direction, 1, 0)
    return face_speed * jnp.where(face_speed > 0, left_state, right_state)


def godunov(fields):
    scalar = fields[0]
    flux_x = face_flux(scalar, fields[1], 0)
    flux_y = face_flux(scalar, fields[2], 1)
    flux_z = face_flux(scalar, fields[3], 2)
    interior = scalar[2:-2, 2:-2, 2:-2]
    updated = interior - courant * ((flux_x[1:] - flux_x[:-1]) + (flux_y[:, 1:] - flux_y[:, :-1]) + (flux_z[:, :, 1:] - flux_z[:, :, :-1]))
    return updated, flux_x, flux_y, flux_z


def double(values):
    return jnp.repeat(jnp.repeat(jnp.repeat(values, 2, axis=1), 2, axis=2), 2, axis=3)


def halves(number, direction):
    offsets = jnp.where(jnp.arange(number) % 2 == 0, -0.25, 0.25).astype(jnp.float32)
    layout = [1, 1, 1, 1]
    layout[direction] = number
    return offsets.reshape(layout)


def refine(coarse_patch):
    center = coarse_patch[:, 1:-1, 1:-1, 1:-1]
    slope_x = 0.5 * (coarse_patch[:, 2:, 1:-1, 1:-1] - coarse_patch[:, :-2, 1:-1, 1:-1])
    slope_y = 0.5 * (coarse_patch[:, 1:-1, 2:, 1:-1] - coarse_patch[:, 1:-1, :-2, 1:-1])
    slope_z = 0.5 * (coarse_patch[:, 1:-1, 1:-1, 2:] - coarse_patch[:, 1:-1, 1:-1, :-2])
    refined = double(center)
    refined = refined + halves(refined.shape[1], 1) * double(slope_x)
    refined = refined + halves(refined.shape[2], 2) * double(slope_y)
    return refined + halves(refined.shape[3], 3) * double(slope_z)


def advance_fine(coarse_patch, own_fields):
    extent_x, extent_y, extent_z = own_fields.shape[1:]
    padded = refine(coarse_patch).at[:, 4:-4, 4:-4, 4:-4].set(own_fields)
    first_new, first_x, first_y, first_z = godunov(padded)
    motion = padded[1:, 2:-2, 2:-2, 2:-2]
    second_new, second_x, second_y, second_z = godunov(jnp.concatenate([first_new[None], motion], 0))
    raw_x = jnp.stack([first_x[2, 2:-2, 2:-2] + second_x[0], first_x[extent_x + 2, 2:-2, 2:-2] + second_x[extent_x]])
    raw_y = jnp.stack([first_y[2:-2, 2, 2:-2] + second_y[:, 0], first_y[2:-2, extent_y + 2, 2:-2] + second_y[:, extent_y]])
    raw_z = jnp.stack([first_z[2:-2, 2:-2, 2] + second_z[:, :, 0], first_z[2:-2, 2:-2, extent_z + 2] + second_z[:, :, extent_z]])
    return second_new, raw_x, raw_y, raw_z


def coarsen(fine_new, raw_x, raw_y, raw_z):
    extent_x, extent_y, extent_z = fine_new.shape
    half_x, half_y, half_z = extent_x // 2, extent_y // 2, extent_z // 2
    average = 0.125 * fine_new.reshape(half_x, 2, half_y, 2, half_z, 2).sum(axis=(1, 3, 5))
    register_x = 0.125 * raw_x.reshape(2, half_y, 2, half_z, 2).sum(axis=(2, 4))
    register_y = 0.125 * raw_y.reshape(2, half_x, 2, half_z, 2).sum(axis=(2, 4))
    register_z = 0.125 * raw_z.reshape(2, half_x, 2, half_y, 2).sum(axis=(2, 4))
    return average, register_x, register_y, register_z


def corrections(flux_x, flux_y, flux_z, corner, registers):
    start_x, start_y, start_z = as_index(corner)
    register_x, register_y, register_z = registers
    half_x, half_y, half_z = register_y.shape[1], register_x.shape[1], register_x.shape[2]
    low_x = lax.dynamic_slice(flux_x, as_index((start_x, start_y, start_z)), (1, half_y, half_z))[0]
    high_x = lax.dynamic_slice(flux_x, as_index((start_x + half_x, start_y, start_z)), (1, half_y, half_z))[0]
    low_y = lax.dynamic_slice(flux_y, as_index((start_x, start_y, start_z)), (half_x, 1, half_z))[:, 0]
    high_y = lax.dynamic_slice(flux_y, as_index((start_x, start_y + half_y, start_z)), (half_x, 1, half_z))[:, 0]
    low_z = lax.dynamic_slice(flux_z, as_index((start_x, start_y, start_z)), (half_x, half_y, 1))[:, :, 0]
    high_z = lax.dynamic_slice(flux_z, as_index((start_x, start_y, start_z + half_z)), (half_x, half_y, 1))[:, :, 0]
    delta_x = courant * (jnp.stack([low_x, high_x]) - register_x)
    delta_y = courant * (jnp.stack([low_y, high_y]) - register_y)
    delta_z = courant * (jnp.stack([low_z, high_z]) - register_z)
    return delta_x, delta_y, delta_z


def apply_child(coarse, corner, average, deltas, active):
    start_x, start_y, start_z = as_index(corner)
    delta_x, delta_y, delta_z = deltas
    half_x, half_y, half_z = average.shape

    def bump(target, anchor, change):
        anchor = as_index(anchor)
        current = lax.dynamic_slice(target, anchor, change.shape)
        return lax.dynamic_update_slice(target, current + jnp.where(active, change, 0.0), anchor)

    coarse = bump(coarse, (start_x - 1, start_y, start_z), delta_x[0][None])
    coarse = bump(coarse, (start_x + half_x, start_y, start_z), -delta_x[1][None])
    coarse = bump(coarse, (start_x, start_y - 1, start_z), delta_y[0][:, None])
    coarse = bump(coarse, (start_x, start_y + half_y, start_z), -delta_y[1][:, None])
    coarse = bump(coarse, (start_x, start_y, start_z - 1), delta_z[0][:, :, None])
    coarse = bump(coarse, (start_x, start_y, start_z + half_z), -delta_z[1][:, :, None])
    anchor = as_index((start_x, start_y, start_z))
    current = lax.dynamic_slice(coarse, anchor, average.shape)
    return lax.dynamic_update_slice(coarse, jnp.where(active, average, current), anchor)


def reference(coarse_scalar, coarse_velocity, coarse_previous, fine_scalar, fine_velocity, fine_previous, parent_shift, offset_y, offset_z):
    coarse_four = jnp.concatenate([coarse_scalar[None], 1.5 * coarse_velocity - 0.5 * coarse_previous], 0)
    padded = jnp.pad(coarse_four, ((0, 0), (2, 2), (2, 2), (2, 2)))
    fine_four = jnp.concatenate([fine_scalar[None], 1.5 * fine_velocity - 0.5 * fine_previous], 0)
    box_count = BOX_ROWS * BOX_COLS

    def coarse_tile(box_index):
        row_index = box_index // BOX_COLS
        col_index = box_index % BOX_COLS
        window = lax.dynamic_slice(padded, as_index((0, row_index * CX, col_index * CY, 0)), (4, CX + 4, CY + 4, CZ + 4))
        return godunov(window)[0]

    stepped = lax.map(coarse_tile, jnp.arange(box_count, dtype=jnp.int32))
    coarse_new = stepped.reshape(BOX_ROWS, BOX_COLS, CX, CY, CZ).transpose(0, 2, 1, 3, 4).reshape(BOX_ROWS * CX, BOX_COLS * CY, CZ)
    columns = jnp.arange(BOX_COLS, dtype=jnp.int32)
    parents = (columns[None, :] + parent_shift).astype(jnp.int32)
    earlier = columns[:, None] > columns[None, :]
    sibling_rank = jnp.sum(((parents[:, :, None] == parents[:, None, :]) & earlier[None]).astype(jnp.int32), axis=2).astype(jnp.int32)
    half_x, half_y, half_z = FX // 2, FY // 2, FZ // 2

    def fine_box(box_index):
        row_index = box_index // BOX_COLS
        col_index = box_index % BOX_COLS
        parent_col = parents[row_index, col_index]
        start_x = (row_index * CX + 1 + (half_x + 2) * sibling_rank[row_index, col_index]).astype(jnp.int32)
        start_y = (parent_col * CY + offset_y[row_index, col_index]).astype(jnp.int32)
        start_z = offset_z[row_index, col_index].astype(jnp.int32)
        coarse_patch = lax.dynamic_slice(padded, as_index((0, start_x - 1, start_y - 1, start_z - 1)), (4, half_x + 6, half_y + 6, half_z + 6))
        own_fields = lax.dynamic_slice(fine_four, as_index((0, row_index * FX, col_index * FY, 0)), (4, FX, FY, FZ))
        fine_new, raw_x, raw_y, raw_z = advance_fine(coarse_patch, own_fields)
        average, register_x, register_y, register_z = coarsen(fine_new, raw_x, raw_y, raw_z)
        unused_scalar, flux_x, flux_y, flux_z = godunov(coarse_patch)
        delta_x, delta_y, delta_z = corrections(flux_x, flux_y, flux_z, (1, 1, 1), (register_x, register_y, register_z))
        return fine_new, average, delta_x, delta_y, delta_z, start_x, start_y, start_z

    fine_all, averages, deltas_x, deltas_y, deltas_z, corner_x, corner_y, corner_z = lax.map(fine_box, jnp.arange(box_count, dtype=jnp.int32))

    def place_child(box_index, coarse):
        corner = (corner_x[box_index], corner_y[box_index], corner_z[box_index])
        deltas = (deltas_x[box_index], deltas_y[box_index], deltas_z[box_index])
        return apply_child(coarse, corner, averages[box_index], deltas, True)

    coarse_result = lax.fori_loop(jnp.int32(0), jnp.int32(box_count), place_child, coarse_new)
    fine_result = fine_all.reshape(BOX_ROWS, BOX_COLS, FX, FY, FZ).transpose(0, 2, 1, 3, 4).reshape(BOX_ROWS * FX, BOX_COLS * FY, FZ)
    return coarse_result, fine_result
```

```python
import jax
import jax.numpy as jnp
from jax import lax
from jax.experimental import pallas as pl
from jax.experimental.pallas import tpu as pltpu
from jax.sharding import PartitionSpec as P

MESH = pl.DeviceIdType.MESH
F32 = jnp.float32
NX = 64
WX = 22
TILES = 5


def minmod(p, q):
    return jnp.maximum(jnp.minimum(p, q), 0.0) + jnp.minimum(jnp.maximum(p, q), 0.0)


def flux(sl, ml, sr, mr, w):
    q = 0.15 * w
    return w * jnp.where(w > 0, sl + (0.5 - q) * ml, sr - (0.5 + q) * mr)


def split_dot(values, matrix):
    high = values.astype(jnp.bfloat16)
    low = (values - high.astype(F32)).astype(jnp.bfloat16)
    return jnp.dot(high, matrix, preferred_element_type=F32) + jnp.dot(low, matrix, preferred_element_type=F32)


def split_dot_left(matrix, values):
    high = values.astype(jnp.bfloat16)
    low = (values - high.astype(F32)).astype(jnp.bfloat16)
    return jnp.dot(matrix, high, preferred_element_type=F32) + jnp.dot(matrix, low, preferred_element_type=F32)


def tile_iota(dim):
    return lax.broadcasted_iota(jnp.int32, (8, 128), dim)


def y_fluxes(s, b):
    d = [s[i + 1] - s[i] for i in range(4)]
    m = [minmod(d[i], d[i + 1]) for i in range(3)]
    low = flux(s[1], m[0], s[2], m[1], b[0] + b[1])
    high = flux(s[2], m[1], s[3], m[2], b[1] + b[2])
    return low, high


def kernel(
    cs, cv, cp, fs, fv, fp, shift, offy, offz,
    out_c, out_f,
    own, partner, xlow, xhigh, ysend, yrecv, slab, msend, mbuf, base, masks,
    gh, fine, s1, s1z, fxs, ry, rz, wavg, wx, vsend, vrecv,
    send_sem, recv_sem,
):
    rows = lax.axis_size("row")
    cols = lax.axis_size("col")
    r = lax.axis_index("row")
    c = lax.axis_index("col")
    core = lax.rem(c, 2)
    j_me = lax.rem(c, 4)
    g0 = c - j_me
    sgn = 2 * core - 1
    r_up = lax.rem(r + 1, rows)
    r_dn = lax.rem(r + rows - 1, rows)
    mate = c + 1 - 2 * core

    def peer(d):
        bit0, bit1 = lax.rem(j_me, 2), j_me // 2
        if d & 1:
            bit0 = 1 - bit0
        if d & 2:
            bit1 = 1 - bit1
        return g0 + 2 * bit1 + bit0

    near = lax.rem(c + sgn + cols, cols)
    far = lax.rem(c + 2 * sgn + cols, cols)

    barrier = pltpu.get_barrier_semaphore()
    greet = [
        (r, peer(1)), (r, peer(2)), (r, peer(3)),
        (r_up, c), (r_dn, c), (r_up, mate), (r_dn, mate),
        (r, near), (r, lax.rem(c + 2, cols)), (r, lax.rem(c + cols - 2, cols)),
    ]
    for dev in greet:
        pl.semaphore_signal(barrier, inc=1, device_id=dev, device_id_type=MESH)

    row = tile_iota(0)
    lane = tile_iota(1)
    l0 = lane == 0
    l127 = lane == 127

    par = [j + shift[0, g0 + j] for j in range(4)]
    oyv = [offy[0, g0 + j] for j in range(4)]
    ozv = [offz[0, g0 + j] for j in range(4)]
    one = jnp.int32(1)
    zero = jnp.int32(0)
    rank = []
    for j in range(4):
        acc = zero
        for i in range(j):
            acc = acc + jnp.where(par[i] == par[j], one, zero)
        rank.append(acc)

    def pick(values, t):
        acc = zero
        for j in range(4):
            acc = acc + jnp.where(t == j, values[j], zero)
        return acc

    def half_coarse(x, carry):
        own[0, x] = cs[x]
        for f in range(3):
            own[f + 1, x] = 0.75 * cv[f, x] - 0.25 * cp[f, x]
        even = [pltpu.roll(own[f, x], 2 * f, 0) if f else own[f, x] for f in range(4)]
        odd = [pltpu.roll(own[f, x], (2 * f + 2) % 8, 0) if f != 3 else own[f, x] for f in range(4)]
        pe, po = even[0], odd[0]
        for f in range(1, 4):
            here = (row >= 2 * f) & (row < 2 * f + 2)
            pe = jnp.where(here, even[f], pe)
            po = jnp.where(here, odd[f], po)
        ysend[x] = jnp.where(core == 0, pe, po)
        return carry

    lax.fori_loop(0, NX, half_coarse, 0)
    pl.semaphore_wait(barrier, len(greet))

    def copy(src, dst, k, dev, kr=None):
        return pltpu.make_async_remote_copy(
            src_ref=src, dst_ref=dst, send_sem=send_sem.at[k], recv_sem=recv_sem.at[k if kr is None else kr],
            device_id=dev, device_id_type=MESH,
        )

    box_copy = copy(own, partner, 0, (r, mate))
    up_copy = copy(own.at[:, pl.ds(NX - 2, 2)], xlow.at[0], 1, (r_up, c))
    up_mate_copy = copy(own.at[:, pl.ds(NX - 2, 2)], xlow.at[1], 2, (r_up, mate))
    down_copy = copy(own.at[:, pl.ds(0, 2)], xhigh, 3, (r_dn, c))
    near_copy = copy(ysend, yrecv.at[1 - core], 4, (r, near), 5 - core)
    far_copy = copy(ysend, yrecv.at[1 - core], 5, (r, far), 5 - core)
    first_copies = (near_copy, far_copy, box_copy, up_copy, up_mate_copy, down_copy)
    for one_copy in first_copies:
        one_copy.start()

    def half_fine(x, carry):
        fine[0, 0, x + 4, pl.ds(4, 8), :] = fs[x]
        for f in range(3):
            fine[f + 1, 0, x + 4, pl.ds(4, 8), :] = 0.75 * fv[f, x] - 0.25 * fp[f, x]
        return carry

    lax.fori_loop(0, 32, half_fine, 0)

    slots = []
    for k in range(3):
        slot, oyk, ozk, valid = zero, zero, zero, zero
        for j in range(4):
            mine = jnp.where((par[j] == j_me) & (rank[j] == k), one, zero)
            dist0 = jnp.where(lax.rem(j_me, 2) == j % 2, zero, one)
            dist1 = jnp.where(j_me // 2 == j // 2, zero, one)
            slot = slot + mine * (dist0 + 2 * dist1)
            oyk = oyk + mine * oyv[j]
            ozk = ozk + mine * ozv[j]
            valid = valid + mine
        slots.append(slot)
        oyk = jnp.where(valid > 0, oyk, -100)
        iny = (row >= oyk) & (row < oyk + 4)
        inz = (lane >= ozk) & (lane < ozk + 64)
        masks[k, 0] = jnp.where((row == oyk - 1) & inz, 0.3, 0.0)
        masks[k, 1] = jnp.where((row == oyk + 4) & inz, 0.3, 0.0)
        masks[k, 2] = jnp.where((lane == ozk - 1) & iny, 0.3, 0.0)
        masks[k, 3] = jnp.where((lane == ozk + 64) & iny, 0.3, 0.0)
        masks[k, 4] = jnp.where(iny & inz, 1.0, 0.0)
    for q in range(5):
        masks[3, q] = jnp.zeros((8, 128), F32)

    base_row = pl.multiple_of(8 + 8 * core, 8)
    mate_row = pl.multiple_of(16 - 8 * core, 8)
    chip = c // 2
    has_low = chip > 0
    has_high = chip < cols // 2 - 1
    row_low = r > 0
    row_high = r < rows - 1

    for h in range(2):
        copy(ysend, yrecv.at[h], 4 + h, (r, near)).wait_recv()
    for k in (0, 1, 2, 3):
        (box_copy, up_copy, up_mate_copy, down_copy)[k].wait_recv()

    def assemble(x, carry):
        for f in range(4):
            slab[f, x + 2, pl.ds(base_row, 8), :] = own[f, x]
            slab[f, x + 2, pl.ds(mate_row, 8), :] = partner[f, x]
            slab[f, x + 2, pl.ds(6, 2), :] = jnp.where(has_low, yrecv[0, x, pl.ds(2 * f, 2), :], 0.0)
            slab[f, x + 2, pl.ds(24, 2), :] = jnp.where(has_high, yrecv[1, x, pl.ds(2 * f, 2), :], 0.0)
        return carry

    lax.fori_loop(0, NX, assemble, 0)
    for f in range(4):
        for i in range(2):
            slab[f, i, pl.ds(base_row, 8), :] = jnp.where(row_low, xlow[0, f, i], 0.0)
            slab[f, i, pl.ds(mate_row, 8), :] = jnp.where(row_low, xlow[1, f, i], 0.0)
            slab[f, NX + 2 + i, pl.ds(base_row, 8), :] = jnp.where(row_high, xhigh[f, i], 0.0)

    def extract(t, store):
        p = pick(par, t)
        first = 18 * pick(rank, t)
        r0 = 5 + 8 * lax.rem(p, 2) + pick(oyv, t)

        def plane(i, carry):
            x = first + i
            store(TILES * i, slab[0, x, pl.ds(r0 + 1, 8), :])
            store(TILES * i + 1, slab[1, x, pl.ds(r0 + 1, 8), :])
            store(TILES * i + 2, slab[2, x, pl.ds(r0 + 1, 8), :])
            store(TILES * i + 3, slab[3, x, pl.ds(r0 + 1, 8), :])
            edge = slab[0, x, pl.ds(r0, 8), :]
            edge = jnp.where(row == 7, slab[0, x, pl.ds(r0 + 2, 8), :], edge)
            edge = jnp.where(row == 1, slab[2, x, pl.ds(r0 - 1, 8), :], edge)
            edge = jnp.where(row == 6, slab[2, x, pl.ds(r0 + 3, 8), :], edge)
            store(TILES * i + 4, edge)
            return carry

        lax.fori_loop(0, WX, plane, 0)

    def store_send(k, value):
        msend[k] = value

    def store_own(k, value):
        mbuf[0, k] = value

    j_cross = lax.rem(j_me + 2, 4)
    extract(j_cross, store_send)
    patch_copy = copy(msend, mbuf.at[1], 6, (r, peer(2)))
    patch_copy.start()
    extract(j_me, store_own)

    def coarse_load(f, x, delta=0):
        return slab[f, x, pl.ds(base_row + delta, 8), :]

    def coarse_plane(x, carry):
        fxl, mx, sx, sn, ax = carry
        snn = coarse_load(0, x + 4)
        an = coarse_load(1, x + 3)
        mn = minmod(sn - sx, snn - sn)
        fxu = flux(sx, mx, sn, mn, ax + an)
        ys = [coarse_load(0, x + 2, d) for d in (-2, -1, 0, 1, 2)]
        yb = [coarse_load(2, x + 2, d) for d in (-1, 0, 1)]
        fyl, fyu = y_fluxes(ys, yb)
        vz = coarse_load(3, x + 2)
        up = jnp.where(l127, 0.0, pltpu.roll(sx, 127, 1))
        dn = jnp.where(l0, 0.0, pltpu.roll(sx, 1, 1))
        mz = minmod(sx - dn, up - sx)
        mu = jnp.where(l127, 0.0, pltpu.roll(mz, 127, 1))
        vu = jnp.where(l127, 0.0, pltpu.roll(vz, 127, 1))
        fzu = flux(sx, mz, up, mu, vz + vu)
        w0 = jnp.minimum(vz, 0.0)
        fzl = jnp.where(l0, w0 * (sx - (0.5 + 0.15 * w0) * mz), pltpu.roll(fzu, 1, 1))
        new = sx - 0.3 * ((fxu - fxl) + (fyu - fyl) + (fzu - fzl))
        k = x // 18
        i = x - 18 * k
        mid = jnp.where((i >= 1) & (i <= 16), 1.0, 0.0).astype(F32)
        lowx = jnp.where(i == 0, 0.3, 0.0).astype(F32)
        highx = jnp.where(i == 17, 0.3, 0.0).astype(F32)
        cov = masks[k, 4]
        new = new + mid * (masks[k, 0] * fyu - masks[k, 1] * fyl + masks[k, 2] * fzu - masks[k, 3] * fzl)
        new = new + cov * (lowx * fxu - highx * fxl)
        base[x] = jnp.where(cov * mid > 0, 0.0, new)
        return fxu, mn, sn, snn, an

    def coarse_pair(h, carry):
        for e in range(2):
            carry = coarse_plane(2 * h + e, carry)
        return carry

    p0, p1, p2, p3 = [coarse_load(0, i) for i in range(4)]
    v1, v2 = coarse_load(1, 1), coarse_load(1, 2)
    m1, m2 = minmod(p1 - p0, p2 - p1), minmod(p2 - p1, p3 - p2)
    lax.fori_loop(0, NX // 2, coarse_pair, (flux(p1, m1, p2, m2, v1 + v2), m2, p2, p3, v2))

    my_par = pick(par, j_me)
    my_oy = pick(oyv, j_me)
    my_oz = pick(ozv, j_me)
    sel = jnp.where(my_par // 2 == j_me // 2, zero, one)
    zi = lax.broadcasted_iota(jnp.int32, (128, 512), 0)
    qi = lax.broadcasted_iota(jnp.int32, (128, 512), 1)
    lq = qi & 127
    cell0 = my_oz + (lq >> 1)
    cell1 = jnp.where(lq < 4, my_oz + 64 + (lq >> 1), jnp.where(lq >= 124, my_oz + ((lq - 128) >> 1), -1000))
    cell = jnp.where((qi & 128) == 0, cell0, cell1)
    slope = jnp.where(qi >= 256, jnp.where((qi & 1) == 0, -0.125, 0.125), 0.0)
    zmat = jnp.where(zi == cell, 1.0, 0.0) + jnp.where(zi == cell + 1, slope, 0.0) - jnp.where(zi == cell - 1, slope, 0.0)
    zmat = zmat.astype(jnp.bfloat16)

    patch_copy.wait_recv()
    half = WX * TILES // 2
    for h in range(2):
        lhs = mbuf[sel, pl.ds(h * half, half)].reshape(half * 8, 128)
        res = split_dot(lhs, zmat)
        for q in range(4):
            gh[q, pl.ds(h * half, half)] = res[:, 128 * q:128 * (q + 1)].reshape(half, 8, 128)

    def refine_plane(i, full):
        for lt in range(2):
            edge = gh[lt, TILES * i + 4]
            for f in range(4):
                g = gh[lt, TILES * i + f]
                sx = 0.125 * (gh[lt, TILES * (i + 1) + f] - gh[lt, TILES * (i - 1) + f])
                lo = pltpu.roll(g, 1, 0)
                hi = pltpu.roll(g, 7, 0)
                if f == 0:
                    lo = jnp.where(row == 0, edge, lo)
                    hi = jnp.where(row == 7, edge, hi)
                if f == 2:
                    lo = jnp.where(row == 0, pltpu.roll(edge, 7, 0), lo)
                    hi = jnp.where(row == 7, pltpu.roll(edge, 1, 0), hi)
                sy = 0.125 * (hi - lo)
                ctr = gh[2 + lt, TILES * i + f]
                for e in range(2):
                    cx = ctr + sx if e else ctr - sx
                    for ey in range(2):
                        value = cx + sy if ey else cx - sy
                        xf = 2 * (i - 1) + e
                        if full or lt == 1:
                            fine[f, lt, xf, pl.ds(ey, 8, stride=2), :] = value
                        else:
                            fine[f, lt, xf, pl.ds(ey, 2, stride=2), :] = value[0:2]
                            fine[f, lt, xf, pl.ds(12 + ey, 2, stride=2), :] = value[6:8]

    def refine_ends(i, carry):
        refine_plane(jnp.where(i < 2, i + 1, i + 17), True)
        return carry

    def refine_middle(i, carry):
        refine_plane(i, False)
        return carry

    lax.fori_loop(0, 4, refine_ends, 0)
    lax.fori_loop(3, 19, refine_middle, 0)

    def zup(t0, t1):
        a0, a1 = pltpu.roll(t0, 127, 1), pltpu.roll(t1, 127, 1)
        return jnp.where(l127, a1, a0), jnp.where(l127, a0, a1)

    def zdn(t0, t1):
        a0, a1 = pltpu.roll(t0, 1, 1), pltpu.roll(t1, 1, 1)
        return jnp.where(l0, a1, a0), jnp.where(l0, a0, a1)

    def z_fluxes(t0, t1, w0, w1):
        u0, u1 = zup(t0, t1)
        d0, d1 = zdn(t0, t1)
        n0, n1 = minmod(t0 - d0, u0 - t0), minmod(t1 - d1, u1 - t1)
        nu0, nu1 = zup(n0, n1)
        wu0, wu1 = zup(w0, w1)
        h0, h1 = flux(t0, n0, u0, nu0, w0 + wu0), flux(t1, n1, u1, nu1, w1 + wu1)
        b0, b1 = zdn(h0, h1)
        return b0, h0, b1, h1

    def load(block, f, x, d=0):
        if block == 0:
            return fine[f, 0, x, pl.ds(4 + d, 8), :]
        if block == 1:
            return fine[f, 1, x, pl.ds(4 + d, 8), :]
        return jnp.where(row < 4, fine[f, 0, x, pl.ds(2 + d, 8), :], fine[f, 0, x, pl.ds(6 + d, 8), :])

    def load_pad(f, x):
        return jnp.where(row < 4, fine[f, 1, x, pl.ds(2, 8), :], fine[f, 1, x, pl.ds(6, 8), :])

    def x_start(block, x):
        a0, a1, a2, a3 = [load(block, 0, x + d) for d in (-2, -1, 0, 1)]
        w0, w1 = load(block, 1, x - 1), load(block, 1, x)
        n1, n2 = minmod(a1 - a0, a2 - a1), minmod(a2 - a1, a3 - a2)
        return flux(a1, n1, a2, n2, w0 + w1), n2, a2, a3, w1

    def x_next(block, x, carry):
        fxl, mx, sx, sn, ax = carry
        snn = load(block, 0, x + 2)
        an = load(block, 1, x + 1)
        mn = minmod(sn - sx, snn - sn)
        fxu = flux(sx, mx, sn, mn, ax + an)
        return fxl, fxu, (fxu, mn, sn, snn, an)

    def first_plane(x, carries):
        out, xs, ys = [], [], []
        for block in range(3):
            fxl, fxu, nxt = x_next(block, x, carries[block])
            out.append(nxt)
            xs.append((fxl, fxu))
            ys.append(y_fluxes([load(block, 0, x, d) for d in (-2, -1, 0, 1, 2)], [load(block, 2, x, d) for d in (-1, 0, 1)]))
        c0, c1, c2 = carries[0][2], carries[1][2], carries[2][2]
        zl0, zu0, zl1, zu1 = z_fluxes(c0, c1, load(0, 3, x), load(1, 3, x))
        zl2, zu2, _, _ = z_fluxes(c2, load_pad(0, x), load(2, 3, x), load_pad(3, x))
        news = []
        for sc, (xl, xu), (yl, yu), (zl, zu) in zip((c0, c1, c2), xs, ys, ((zl0, zu0), (zl1, zu1), (zl2, zu2))):
            news.append(sc - 0.3 * ((xu - xl) + (yu - yl) + (zu - zl)))
        s1[x - 2, pl.ds(2, 8), :] = news[0]
        s1[x - 2, pl.ds(0, 2), :] = news[2][0:2]
        s1[x - 2, pl.ds(10, 2), :] = news[2][6:8]
        s1z[x - 2] = news[1]
        reg_y = jnp.where(row == 0, ys[0][0], jnp.where(row == 7, ys[0][1], 0.0))
        reg_z = jnp.where(l0, zl0, jnp.where(l127, zu0, 0.0))
        return tuple(out), reg_y, reg_z, xs[0][1]

    def first_pair(h, carries):
        carries, ya, za, _ = first_plane(2 + 2 * h, carries)
        carries, yb, zb, fx = first_plane(3 + 2 * h, carries)
        ry[h] = ya + yb
        rz[h] = za + zb
        fxs[h] = fx
        return carries

    lax.fori_loop(0, 18, first_pair, tuple(x_start(block, 2) for block in range(3)))

    def second_load(x, d=0):
        return s1[x + 2, pl.ds(2 + d, 8), :]

    def second_plane(x, carry):
        fxl, mx, sx, sn, ax = carry
        snn = second_load(x + 2)
        an = load(0, 1, x + 5)
        mn = minmod(sn - sx, snn - sn)
        fxu = flux(sx, mx, sn, mn, ax + an)
        yl, yu = y_fluxes([second_load(x, d) for d in (-2, -1, 0, 1, 2)], [load(0, 2, x + 4, d) for d in (-1, 0, 1)])
        zl, zu, _, _ = z_fluxes(sx, s1z[x + 2], load(0, 3, x + 4), load(1, 3, x + 4))
        new = sx - 0.3 * ((fxu - fxl) + (yu - yl) + (zu - zl))
        out_f[x] = new
        reg_y = jnp.where(row == 0, yl, jnp.where(row == 7, yu, 0.0))
        reg_z = jnp.where(l0, zl, jnp.where(l127, zu, 0.0))
        return (fxu, mn, sn, snn, an), new, reg_y, reg_z

    def second_pair(h, carry):
        carry, na, ya, za = second_plane(2 * h, carry)
        carry, nb, yb, zb = second_plane(2 * h + 1, carry)
        at = pl.ds(pl.multiple_of(8 * h, 8), 8)
        wavg[0, at, :] = 0.125 * (na + nb)
        wavg[1, at, :] = 0.0375 * (rz[h + 1] + (za + zb))
        wavg[2, at, :] = 0.0375 * (ry[h + 1] + (ya + yb))
        return carry

    q0, q1, q2, q3 = [second_load(i) for i in (-2, -1, 0, 1)]
    u1, u2 = load(0, 1, 3), load(0, 1, 4)
    k1, k2 = minmod(q1 - q0, q2 - q1), minmod(q2 - q1, q3 - q2)
    x_low = flux(q1, k1, q2, k2, u1 + u2)
    x_high = lax.fori_loop(0, 16, second_pair, (x_low, k2, q2, q3, u2))[0]
    wx[...] = jnp.zeros((128, 128), F32)
    wx[pl.ds(0, 8), :] = -0.0375 * (fxs[0] + x_low)
    wx[pl.ds(8, 8), :] = 0.0375 * (fxs[16] + x_high)

    ri = lax.broadcasted_iota(jnp.int32, (128, 128), 0)
    ci = lax.broadcasted_iota(jnp.int32, (128, 128), 1)
    to_z = jnp.where(ci == my_oz + (ri >> 1), 1.0, 0.0).astype(jnp.bfloat16)
    to_zface = jnp.where((ri == 127) & (ci == my_oz + 64), 1.0, 0.0) - jnp.where((ri == 0) & (ci == my_oz - 1), 1.0, 0.0)
    to_zface = to_zface.astype(jnp.bfloat16)
    same = (ri >> 3) == (ci >> 3)
    yr, yc = ri & 7, ci & 7
    to_y = jnp.where(same & (yr == my_oy + (yc >> 1)), 1.0, 0.0).astype(jnp.bfloat16)
    to_yface = jnp.where(same & (yc == 7) & (yr == my_oy + 4), 1.0, 0.0) - jnp.where(same & (yc == 0) & (yr == my_oy - 1), 1.0, 0.0)
    to_yface = to_yface.astype(jnp.bfloat16)
    placed = split_dot(wavg[0], to_z) + split_dot(wavg[1], to_zface)
    faces = split_dot(wavg[2], to_z)
    ends = split_dot(wx[...], to_z)
    middle = split_dot_left(to_y, placed) + split_dot_left(to_yface, faces)
    ends = split_dot_left(to_y, ends)
    vsend[pl.ds(1, 16)] = middle.reshape(16, 8, 128)
    vsend[0] = ends[0:8]
    vsend[17] = ends[8:16]

    back = [copy(vsend, vrecv.at[d], 6 + d, (r, peer(d))) for d in (1, 2, 3)]
    for one_copy in back:
        one_copy.start()
    vrecv[0] = jnp.zeros((18, 8, 128), F32)

    def tail(x, carry):
        out_c[x] = base[x]
        return carry

    lax.fori_loop(54, NX, tail, 0)
    for one_copy in back:
        one_copy.wait_recv()
    for k in range(3):
        def finish(i, carry, k=k):
            out_c[18 * k + i] = base[18 * k + i] + vrecv[slots[k], i]
            return carry

        lax.fori_loop(0, 18, finish, 0)
    for one_copy in first_copies + (patch_copy,) + tuple(back):
        one_copy.wait_send()


def per_device(*args):
    vmem = pl.BlockSpec(memory_space=pltpu.VMEM)
    smem = pl.BlockSpec(memory_space=pltpu.SMEM)

    def buf(*shape):
        return pltpu.VMEM(shape + (8, 128), F32)

    return pl.pallas_call(
        kernel,
        out_shape=(
            jax.ShapeDtypeStruct((64, 8, 128), F32),
            jax.ShapeDtypeStruct((32, 8, 128), F32),
        ),
        in_specs=[vmem] * 6 + [smem] * 3,
        out_specs=(vmem, vmem),
        scratch_shapes=[
            buf(4, NX),
            buf(4, NX),
            buf(2, 4, 2),
            buf(4, 2),
            buf(NX),
            buf(2, NX),
            pltpu.VMEM((4, NX + 4, 32, 128), F32),
            buf(WX * TILES),
            buf(2, WX * TILES),
            buf(NX),
            buf(4, 5),
            buf(4, WX * TILES),
            pltpu.VMEM((4, 2, 40, 16, 128), F32),
            pltpu.VMEM((36, 16, 128), F32),
            buf(36),
            buf(18),
            buf(18),
            buf(18),
            pltpu.VMEM((3, 128, 128), F32),
            pltpu.VMEM((128, 128), F32),
            buf(18),
            buf(4, 18),
            pltpu.SemaphoreType.DMA((10,)),
            pltpu.SemaphoreType.DMA((10,)),
        ],
        compiler_params=pltpu.CompilerParams(
            collective_id=0, has_side_effects=True, vmem_limit_bytes=48 * 1024 * 1024
        ),
    )(*args)


def solution(mesh):
    in_specs = (
        P("row", "col", None),
        P(None, "row", "col", None),
        P(None, "row", "col", None),
        P("row", "col", None),
        P(None, "row", "col", None),
        P(None, "row", "col", None),
        P("row", None),
        P("row", None),
        P("row", None),
    )
    out_specs = (P("row", "col", None), P("row", "col", None))
    return jax.shard_map(
        per_device, mesh=mesh, in_specs=in_specs, out_specs=out_specs, check_vma=False
    )
```

```python
import jax
import jax.numpy as jnp
from jax import lax
from jax.experimental import pallas as pl
from jax.experimental.pallas import tpu as pltpu
from jax.sharding import PartitionSpec as P

MESH = pl.DeviceIdType.MESH
F32 = jnp.float32
NX = 64
WX = 22
TILES = 5
PACK = 3


def minmod(p, q):
    return jnp.maximum(jnp.minimum(p, q), 0.0) + jnp.minimum(jnp.maximum(p, q), 0.0)


def flux(sl, ml, sr, mr, w):
    q = 0.15 * w
    return w * jnp.where(w > 0, sl + (0.5 - q) * ml, sr - (0.5 + q) * mr)


def split_dot(values, matrix):
    high = values.astype(jnp.bfloat16)
    low = (values - high.astype(F32)).astype(jnp.bfloat16)
    return jnp.dot(high, matrix, preferred_element_type=F32) + jnp.dot(low, matrix, preferred_element_type=F32)


def split_dot_left(matrix, values):
    high = values.astype(jnp.bfloat16)
    low = (values - high.astype(F32)).astype(jnp.bfloat16)
    return jnp.dot(matrix, high, preferred_element_type=F32) + jnp.dot(matrix, low, preferred_element_type=F32)


def tile_iota(dim):
    return lax.broadcasted_iota(jnp.int32, (8, 128), dim)


def y_fluxes(s, b):
    d = [s[i + 1] - s[i] for i in range(4)]
    m = [minmod(d[i], d[i + 1]) for i in range(3)]
    low = flux(s[1], m[0], s[2], m[1], b[0] + b[1])
    high = flux(s[2], m[1], s[3], m[2], b[1] + b[2])
    return low, high


def kernel(
    cs_h, cv_h, cp_h, fs_h, fv_h, fp_h, shift_h, offy_h, offz_h,
    out_c, out_f,
    cs, cv, cp, fs, fv, fp, shift, offy, offz,
    own, partner, xlow, xhigh, ysend, yrecv, slab, msend, mbuf, wide, base, masks,
    gh, fine, s1, s1z, fxs, ry, rz, wavg, wx, vsend, vrecv,
    load_sem, send_sem, recv_sem, ready,
):
    rows = lax.axis_size("row")
    cols = lax.axis_size("col")
    r = lax.axis_index("row")
    c = lax.axis_index("col")
    core = lax.rem(c, 2)
    j_me = lax.rem(c, 4)
    g0 = c - j_me
    sgn = 2 * core - 1
    mate = c + 1 - 2 * core
    chip = c // 2
    has_low = chip > 0
    has_high = chip < cols // 2 - 1
    row_low = r > 0
    row_high = r < rows - 1
    has_side = jnp.where(core == 0, has_low, has_high)
    out_dir = jnp.where(j_me < 2, -1, 1)
    has_out = jnp.where(j_me < 2, has_low, has_high)
    outer = (j_me == 0) | (j_me == 3)

    loads = [pltpu.make_async_copy(src, dst, load_sem.at[k]) for k, (src, dst) in enumerate(
        [(shift_h, shift), (offy_h, offy), (offz_h, offz), (cs_h, cs)]
        + [(cv_h.at[f], cv.at[f]) for f in range(3)] + [(cp_h.at[f], cp.at[f]) for f in range(3)]
        + [(fs_h, fs)] + [(fv_h.at[f], fv.at[f]) for f in range(3)] + [(fp_h.at[f], fp.at[f]) for f in range(3)]
    )]
    for load_copy in loads:
        load_copy.start()

    def peer(d):
        bit0, bit1 = lax.rem(j_me, 2), j_me // 2
        if d & 1:
            bit0 = 1 - bit0
        if d & 2:
            bit1 = 1 - bit1
        return g0 + 2 * bit1 + bit0

    near = c + sgn
    far = c + 2 * sgn

    barrier = pltpu.get_barrier_semaphore()

    def greet(*dev):
        pl.semaphore_signal(barrier, inc=1, device_id=dev, device_id_type=MESH)

    for d in (1, 2, 3):
        greet(r, peer(d))

    @pl.when(has_out)
    def _():
        greet(r, c + 2 * out_dir)

    @pl.when(has_out & outer)
    def _():
        greet(r, c + out_dir)

    @pl.when(row_high)
    def _():
        greet(r + 1, c)
        greet(r + 1, mate)

    row = tile_iota(0)
    lane = tile_iota(1)
    l0 = lane == 0
    l127 = lane == 127

    for k in range(3):
        loads[k].wait()
    par = [j + shift[0, g0 + j] for j in range(4)]
    oyv = [offy[0, g0 + j] for j in range(4)]
    ozv = [offz[0, g0 + j] for j in range(4)]
    one = jnp.int32(1)
    zero = jnp.int32(0)
    rank = []
    for j in range(4):
        acc = zero
        for i in range(j):
            acc = acc + jnp.where(par[i] == par[j], one, zero)
        rank.append(acc)

    def pick(values, t):
        acc = zero
        for j in range(4):
            acc = acc + jnp.where(t == j, values[j], zero)
        return acc

    def half_plane(x):
        values = [cs[x]] + [0.75 * cv[f, x] - 0.25 * cp[f, x] for f in range(3)]
        for f in range(4):
            own[f, x] = values[f]
        return values

    def rows_at(value, at):
        return jnp.where(core == 0, pltpu.roll(value, at, 0) if at else value, pltpu.roll(value, (at + 2) % 8, 0))

    def half_coarse(h, carry):
        planes = [half_plane(4 * h + e) for e in range(4)]
        for t in range(2):
            tile = rows_at(planes[2 * t][0], 0)
            for k, value in ((2, planes[2 * t][2]), (4, planes[2 * t + 1][0]), (6, planes[2 * t + 1][2])):
                tile = jnp.where(row >= k, rows_at(value, k), tile)
            ysend[3 * h + t] = tile
        tile = None
        for e in range(4):
            for q in range(2):
                value, at = planes[e][2 * q + 1], 2 * e + q
                moved = jnp.where(core == 0, pltpu.roll(value, at, 0) if at else value, pltpu.roll(value, (at + 1) % 8, 0))
                tile = moved if tile is None else jnp.where(row >= at, moved, tile)
        ysend[3 * h + 2] = tile
        return carry

    for k in range(3, 10):
        loads[k].wait()
    lax.fori_loop(0, NX // 4, half_coarse, 0)

    greeters = 3 + jnp.where(has_out, jnp.where(outer, 2, 1), 0) + jnp.where(row_low, 2, 0)
    pl.semaphore_wait(barrier, greeters)

    def copy(src, dst, k, dev, kr=None):
        return pltpu.make_async_remote_copy(
            src_ref=src, dst_ref=dst, send_sem=send_sem.at[k], recv_sem=recv_sem.at[k if kr is None else kr],
            device_id=dev, device_id_type=MESH,
        )

    box_copy = copy(own, partner, 0, (r, mate))
    up_copy = copy(own.at[:, pl.ds(NX - 2, 2)], xlow.at[0], 1, (r + 1, c))
    up_mate_copy = copy(own.at[:, pl.ds(NX - 2, 2)], xlow.at[1], 2, (r + 1, mate))
    down_copy = copy(own.at[pl.ds(0, 2), pl.ds(0, 2)], xhigh, 3, (r - 1, c))
    near_copy = copy(ysend, yrecv.at[1 - core], 4, (r, near), 5 - core)
    far_copy = copy(ysend, yrecv.at[1 - core], 5, (r, far), 5 - core)

    @pl.when(has_side)
    def _():
        near_copy.start()
        far_copy.start()

    box_copy.start()

    @pl.when(row_low)
    def _():
        pl.semaphore_signal(ready, inc=1, device_id=(r - 1, c), device_id_type=MESH)
        pl.semaphore_signal(ready, inc=1, device_id=(r - 1, mate), device_id_type=MESH)
        down_copy.start()

    def half_fine(x, carry):
        fine[0, 0, x + 4, pl.ds(4, 8), :] = fs[x]
        for f in range(3):
            fine[f + 1, 0, x + 4, pl.ds(4, 8), :] = 0.75 * fv[f, x] - 0.25 * fp[f, x]
        return carry

    for k in range(10, 17):
        loads[k].wait()
    lax.fori_loop(0, 32, half_fine, 0, unroll=4)

    slots = []
    for k in range(3):
        slot, oyk, ozk, valid = zero, zero, zero, zero
        for j in range(4):
            mine = jnp.where((par[j] == j_me) & (rank[j] == k), one, zero)
            dist0 = jnp.where(lax.rem(j_me, 2) == j % 2, zero, one)
            dist1 = jnp.where(j_me // 2 == j // 2, zero, one)
            slot = slot + mine * (dist0 + 2 * dist1)
            oyk = oyk + mine * oyv[j]
            ozk = ozk + mine * ozv[j]
            valid = valid + mine
        slots.append(slot)
        oyk = jnp.where(valid > 0, oyk, -100)
        iny = (row >= oyk) & (row < oyk + 4)
        inz = (lane >= ozk) & (lane < ozk + 64)
        masks[k, 0] = jnp.where((row == oyk - 1) & inz, 0.3, 0.0)
        masks[k, 1] = jnp.where((row == oyk + 4) & inz, 0.3, 0.0)
        masks[k, 2] = jnp.where((lane == ozk - 1) & iny, 0.3, 0.0)
        masks[k, 3] = jnp.where((lane == ozk + 64) & iny, 0.3, 0.0)
        masks[k, 4] = jnp.where(iny & inz, 1.0, 0.0)
    for q in range(5):
        masks[3, q] = jnp.zeros((8, 128), F32)

    base_row = pl.multiple_of(8 + 8 * core, 8)
    mate_row = pl.multiple_of(16 - 8 * core, 8)

    @pl.when(has_low)
    def _():
        copy(ysend, yrecv.at[0], 4, (r, mate)).wait_recv()

    @pl.when(has_high)
    def _():
        copy(ysend, yrecv.at[1], 5, (r, mate)).wait_recv()

    for side, has in ((0, has_low), (1, has_high)):
        @pl.when(jnp.logical_not(has))
        def _(side=side):
            yrecv[side] = jnp.zeros((3 * NX // 4, 8, 128), F32)

    box_copy.wait_recv()

    def assemble(h, carry):
        for e in range(4):
            x = 4 * h + e
            for f in range(4):
                slab[f, x + 2, pl.ds(base_row, 8), :] = own[f, x]
                slab[f, x + 2, pl.ds(mate_row, 8), :] = partner[f, x]
            for side, at in ((0, 6), (1, 24)):
                pair = 3 * h + e // 2
                slab[0, x + 2, pl.ds(at, 2), :] = yrecv[side, pair, pl.ds(4 * (e % 2), 2), :]
                slab[2, x + 2, pl.ds(at, 2), :] = yrecv[side, pair, pl.ds(4 * (e % 2) + 2, 2), :]
                alone = 7 if side == 0 else 24
                slab[1, x + 2, pl.ds(alone, 1), :] = yrecv[side, 3 * h + 2, pl.ds(2 * e, 1), :]
                slab[3, x + 2, pl.ds(alone, 1), :] = yrecv[side, 3 * h + 2, pl.ds(2 * e + 1, 1), :]
        return carry

    lax.fori_loop(0, NX // 4, assemble, 0)

    def extractor(t, store):
        p = pick(par, t)
        first = 18 * pick(rank, t)
        r0 = 5 + 8 * lax.rem(p, 2) + pick(oyv, t)
        turn = 131 - pick(ozv, t)

        def plane(i, carry):
            x = first + i

            def rolled(value, to):
                return pltpu.roll(value, lax.rem(turn + to, 128), 1)

            four = [slab[f, x, pl.ds(r0 + 1, 8), :] for f in range(4)]
            edge = slab[0, x, pl.ds(r0, 8), :]
            edge = jnp.where(row == 7, slab[0, x, pl.ds(r0 + 2, 8), :], edge)
            edge = jnp.where(row == 1, slab[2, x, pl.ds(r0 - 1, 8), :], edge)
            edge = jnp.where(row == 6, slab[2, x, pl.ds(r0 + 3, 8), :], edge)
            rest = rolled(edge, 0)
            for f in range(4):
                rest = jnp.where(lane >= 96 + 8 * f, rolled(four[f], 32 + 8 * f), rest)
            store(PACK * i, jnp.where(lane < 64, rolled(four[0], 0), rolled(four[1], 64)))
            store(PACK * i + 1, jnp.where(lane < 64, rolled(four[2], 0), rolled(four[3], 64)))
            store(PACK * i + 2, rest)
            return carry

        return plane

    def store_send(k, value):
        msend[k] = value

    def store_own(k, value):
        mbuf[0, k] = value

    cut = 2 * PACK
    size = (WX - 2) * PACK
    cross = extractor(lax.rem(j_me + 2, 4), store_send)
    lax.fori_loop(2, WX, cross, 0, unroll=4)
    patch_copy = copy(msend.at[pl.ds(cut, size)], mbuf.at[1, pl.ds(cut, size)], 6, (r, peer(2)))
    patch_copy.start()

    @pl.when(row_high)
    def _():
        pl.semaphore_wait(ready, 2)
        up_copy.start()
        up_mate_copy.start()

    mine = extractor(j_me, store_own)
    lax.fori_loop(2, WX, mine, 0, unroll=4)

    @pl.when(row_low)
    def _():
        up_copy.wait_recv()
        up_mate_copy.wait_recv()
        for f in range(4):
            for i in range(2):
                slab[f, i, pl.ds(base_row, 8), :] = xlow[0, f, i]
                slab[f, i, pl.ds(mate_row, 8), :] = xlow[1, f, i]

    @pl.when(jnp.logical_not(row_low))
    def _():
        for f in range(4):
            for i in range(2):
                slab[f, i] = jnp.zeros((32, 128), F32)

    for i in range(2):
        cross(i, 0)
    start_copy = copy(msend.at[pl.ds(0, cut)], mbuf.at[1, pl.ds(0, cut)], 10, (r, peer(2)))
    start_copy.start()
    for i in range(2):
        mine(i, 0)

    def coarse_load(f, x, delta=0):
        return slab[f, x, pl.ds(base_row + delta, 8), :]

    def coarse_plane(x, carry):
        fxl, mx, sx, sn, ax = carry
        snn = coarse_load(0, x + 4)
        an = coarse_load(1, x + 3)
        mn = minmod(sn - sx, snn - sn)
        fxu = flux(sx, mx, sn, mn, ax + an)
        ys = [coarse_load(0, x + 2, d) for d in (-2, -1, 0, 1, 2)]
        yb = [coarse_load(2, x + 2, d) for d in (-1, 0, 1)]
        fyl, fyu = y_fluxes(ys, yb)
        vz = coarse_load(3, x + 2)
        up = jnp.where(l127, 0.0, pltpu.roll(sx, 127, 1))
        dn = jnp.where(l0, 0.0, pltpu.roll(sx, 1, 1))
        mz = minmod(sx - dn, up - sx)
        mu = jnp.where(l127, 0.0, pltpu.roll(mz, 127, 1))
        vu = jnp.where(l127, 0.0, pltpu.roll(vz, 127, 1))
        fzu = flux(sx, mz, up, mu, vz + vu)
        w0 = jnp.minimum(vz, 0.0)
        fzl = jnp.where(l0, w0 * (sx - (0.5 + 0.15 * w0) * mz), pltpu.roll(fzu, 1, 1))
        new = sx - 0.3 * ((fxu - fxl) + (fyu - fyl) + (fzu - fzl))
        k = x // 18
        i = x - 18 * k
        mid = jnp.where((i >= 1) & (i <= 16), 1.0, 0.0).astype(F32)
        lowx = jnp.where(i == 0, 0.3, 0.0).astype(F32)
        highx = jnp.where(i == 17, 0.3, 0.0).astype(F32)
        cov = masks[k, 4]
        new = new + mid * (masks[k, 0] * fyu - masks[k, 1] * fyl + masks[k, 2] * fzu - masks[k, 3] * fzl)
        new = new + cov * (lowx * fxu - highx * fxl)
        base[x] = jnp.where(cov * mid > 0, 0.0, new)
        return fxu, mn, sn, snn, an

    def coarse_group(h, carry):
        for e in range(6):
            carry = coarse_plane(6 * h + e, carry)
        return carry

    def coarse_start(x):
        p0, p1, p2, p3 = [coarse_load(0, x + i) for i in range(4)]
        v1, v2 = coarse_load(1, x + 1), coarse_load(1, x + 2)
        m1, m2 = minmod(p1 - p0, p2 - p1), minmod(p2 - p1, p3 - p2)
        return flux(p1, m1, p2, m2, v1 + v2), m2, p2, p3, v2

    coarse_carry = lax.fori_loop(0, 10, coarse_group, coarse_start(0))
    for x in (60, 61):
        coarse_carry = coarse_plane(jnp.int32(x), coarse_carry)

    my_par = pick(par, j_me)
    my_oy = pick(oyv, j_me)
    my_oz = pick(ozv, j_me)
    sel = jnp.where(my_par // 2 == j_me // 2, zero, one)
    zi = lax.broadcasted_iota(jnp.int32, (128, 512), 0)
    qi = lax.broadcasted_iota(jnp.int32, (128, 512), 1)
    lq = qi & 127
    cell0 = my_oz + (lq >> 1)
    cell1 = jnp.where(lq < 4, my_oz + 64 + (lq >> 1), jnp.where(lq >= 124, my_oz + ((lq - 128) >> 1), -1000))
    cell = jnp.where((qi & 128) == 0, cell0, cell1)
    slope = jnp.where(qi >= 256, jnp.where((qi & 1) == 0, -0.125, 0.125), 0.0)
    zi = jnp.where((zi < 70) & (zi + my_oz >= 3) & (zi + my_oz < 131), zi + my_oz - 3, -5000)
    zmat = jnp.where(zi == cell, 1.0, 0.0) + jnp.where(zi == cell + 1, slope, 0.0) - jnp.where(zi == cell - 1, slope, 0.0)
    zmat = zmat.astype(jnp.bfloat16)

    patch_copy.wait_recv()
    start_copy.wait_recv()

    def unpack(i, carry):
        first, second, rest = [mbuf[sel, PACK * i + q] for q in range(PACK)]
        for f, value in enumerate((first, pltpu.roll(first, 64, 1), second, pltpu.roll(second, 64, 1))):
            wide[TILES * i + f] = jnp.where(lane < 64, value, pltpu.roll(rest, 96 - 8 * f, 1))
        wide[TILES * i + 4] = rest
        return carry

    lax.fori_loop(0, WX, unpack, 0, unroll=2)
    half = WX * TILES // 2
    for h in range(2):
        lhs = wide[pl.ds(h * half, half)].reshape(half * 8, 128)
        res = split_dot(lhs, zmat)
        for q in range(4):
            gh[q, pl.ds(h * half, half)] = res[:, 128 * q:128 * (q + 1)].reshape(half, 8, 128)

    def refine_plane(i, full):
        for lt in range(2):
            edge = gh[lt, TILES * i + 4]
            for f in range(4):
                g = gh[lt, TILES * i + f]
                sx = 0.125 * (gh[lt, TILES * (i + 1) + f] - gh[lt, TILES * (i - 1) + f])
                lo = pltpu.roll(g, 1, 0)
                hi = pltpu.roll(g, 7, 0)
                if f == 0:
                    lo = jnp.where(row == 0, edge, lo)
                    hi = jnp.where(row == 7, edge, hi)
                if f == 2:
                    lo = jnp.where(row == 0, pltpu.roll(edge, 7, 0), lo)
                    hi = jnp.where(row == 7, pltpu.roll(edge, 1, 0), hi)
                sy = 0.125 * (hi - lo)
                ctr = gh[2 + lt, TILES * i + f]
                for e in range(2):
                    cx = ctr + sx if e else ctr - sx
                    for ey in range(2):
                        value = cx + sy if ey else cx - sy
                        xf = 2 * (i - 1) + e
                        if full or lt == 1:
                            fine[f, lt, xf, pl.ds(ey, 8, stride=2), :] = value
                        else:
                            fine[f, lt, xf, pl.ds(ey, 2, stride=2), :] = value[0:2]
                            fine[f, lt, xf, pl.ds(12 + ey, 2, stride=2), :] = value[6:8]

    def refine_ends(i, carry):
        refine_plane(jnp.where(i < 2, i + 1, i + 17), True)
        return carry

    def refine_middle(i, carry):
        refine_plane(i, False)
        return carry

    lax.fori_loop(0, 4, refine_ends, 0)
    lax.fori_loop(3, 19, refine_middle, 0)

    def zup(t0, t1):
        a0, a1 = pltpu.roll(t0, 127, 1), pltpu.roll(t1, 127, 1)
        return jnp.where(l127, a1, a0), jnp.where(l127, a0, a1)

    def zdn(t0, t1):
        a0, a1 = pltpu.roll(t0, 1, 1), pltpu.roll(t1, 1, 1)
        return jnp.where(l0, a1, a0), jnp.where(l0, a0, a1)

    def z_fluxes(t0, t1, w0, w1):
        u0, u1 = zup(t0, t1)
        d0, d1 = zdn(t0, t1)
        n0, n1 = minmod(t0 - d0, u0 - t0), minmod(t1 - d1, u1 - t1)
        nu0, nu1 = zup(n0, n1)
        wu0, wu1 = zup(w0, w1)
        h0, h1 = flux(t0, n0, u0, nu0, w0 + wu0), flux(t1, n1, u1, nu1, w1 + wu1)
        b0, b1 = zdn(h0, h1)
        return b0, h0, b1, h1

    def load(block, f, x, d=0):
        if block == 0:
            return fine[f, 0, x, pl.ds(4 + d, 8), :]
        if block == 1:
            return fine[f, 1, x, pl.ds(4 + d, 8), :]
        return jnp.where(row < 4, fine[f, 0, x, pl.ds(2 + d, 8), :], fine[f, 0, x, pl.ds(6 + d, 8), :])

    def load_pad(f, x):
        return jnp.where(row < 4, fine[f, 1, x, pl.ds(2, 8), :], fine[f, 1, x, pl.ds(6, 8), :])

    def x_start(block, x):
        a0, a1, a2, a3 = [load(block, 0, x + d) for d in (-2, -1, 0, 1)]
        w0, w1 = load(block, 1, x - 1), load(block, 1, x)
        n1, n2 = minmod(a1 - a0, a2 - a1), minmod(a2 - a1, a3 - a2)
        return flux(a1, n1, a2, n2, w0 + w1), n2, a2, a3, w1

    def x_next(block, x, carry):
        fxl, mx, sx, sn, ax = carry
        snn = load(block, 0, x + 2)
        an = load(block, 1, x + 1)
        mn = minmod(sn - sx, snn - sn)
        fxu = flux(sx, mx, sn, mn, ax + an)
        return fxl, fxu, (fxu, mn, sn, snn, an)

    def first_plane(x, carries):
        out, xs, ys = [], [], []
        for block in range(3):
            fxl, fxu, nxt = x_next(block, x, carries[block])
            out.append(nxt)
            xs.append((fxl, fxu))
            ys.append(y_fluxes([load(block, 0, x, d) for d in (-2, -1, 0, 1, 2)], [load(block, 2, x, d) for d in (-1, 0, 1)]))
        c0, c1, c2 = carries[0][2], carries[1][2], carries[2][2]
        zl0, zu0, zl1, zu1 = z_fluxes(c0, c1, load(0, 3, x), load(1, 3, x))
        zl2, zu2, _, _ = z_fluxes(c2, load_pad(0, x), load(2, 3, x), load_pad(3, x))
        news = []
        for sc, (xl, xu), (yl, yu), (zl, zu) in zip((c0, c1, c2), xs, ys, ((zl0, zu0), (zl1, zu1), (zl2, zu2))):
            news.append(sc - 0.3 * ((xu - xl) + (yu - yl) + (zu - zl)))
        s1[x - 2, pl.ds(2, 8), :] = news[0]
        s1[x - 2, pl.ds(0, 2), :] = news[2][0:2]
        s1[x - 2, pl.ds(10, 2), :] = news[2][6:8]
        s1z[x - 2] = news[1]
        reg_y = jnp.where(row == 0, ys[0][0], jnp.where(row == 7, ys[0][1], 0.0))
        reg_z = jnp.where(l0, zl0, jnp.where(l127, zu0, 0.0))
        return tuple(out), reg_y, reg_z, xs[0][1]

    def first_pair(h, carries):
        carries, ya, za, _ = first_plane(2 + 2 * h, carries)
        carries, yb, zb, fx = first_plane(3 + 2 * h, carries)
        ry[h] = ya + yb
        rz[h] = za + zb
        fxs[h] = fx
        return carries

    def first_group(h, carries):
        for e in range(3):
            carries = first_pair(3 * h + e, carries)
        return carries

    lax.fori_loop(0, 6, first_group, tuple(x_start(block, 2) for block in range(3)))

    def second_load(x, d=0):
        return s1[x + 2, pl.ds(2 + d, 8), :]

    def second_plane(x, carry):
        fxl, mx, sx, sn, ax = carry
        snn = second_load(x + 2)
        an = load(0, 1, x + 5)
        mn = minmod(sn - sx, snn - sn)
        fxu = flux(sx, mx, sn, mn, ax + an)
        yl, yu = y_fluxes([second_load(x, d) for d in (-2, -1, 0, 1, 2)], [load(0, 2, x + 4, d) for d in (-1, 0, 1)])
        zl, zu, _, _ = z_fluxes(sx, s1z[x + 2], load(0, 3, x + 4), load(1, 3, x + 4))
        new = sx - 0.3 * ((fxu - fxl) + (yu - yl) + (zu - zl))
        out_f[x] = new
        reg_y = jnp.where(row == 0, yl, jnp.where(row == 7, yu, 0.0))
        reg_z = jnp.where(l0, zl, jnp.where(l127, zu, 0.0))
        return (fxu, mn, sn, snn, an), new, reg_y, reg_z

    def second_pair(h, carry):
        carry, na, ya, za = second_plane(2 * h, carry)
        carry, nb, yb, zb = second_plane(2 * h + 1, carry)
        at = pl.ds(pl.multiple_of(8 * h, 8), 8)
        wavg[0, at, :] = 0.125 * (na + nb)
        wavg[1, at, :] = 0.0375 * (rz[h + 1] + (za + zb))
        wavg[2, at, :] = 0.0375 * (ry[h + 1] + (ya + yb))
        return carry

    q0, q1, q2, q3 = [second_load(i) for i in (-2, -1, 0, 1)]
    u1, u2 = load(0, 1, 3), load(0, 1, 4)
    k1, k2 = minmod(q1 - q0, q2 - q1), minmod(q2 - q1, q3 - q2)
    x_low = flux(q1, k1, q2, k2, u1 + u2)
    def second_group(h, carry):
        for e in range(4):
            carry = second_pair(4 * h + e, carry)
        return carry

    x_high = lax.fori_loop(0, 4, second_group, (x_low, k2, q2, q3, u2))[0]
    wx[...] = jnp.zeros((128, 128), F32)
    wx[pl.ds(0, 8), :] = -0.0375 * (fxs[0] + x_low)
    wx[pl.ds(8, 8), :] = 0.0375 * (fxs[16] + x_high)

    ri = lax.broadcasted_iota(jnp.int32, (128, 128), 0)
    ci = lax.broadcasted_iota(jnp.int32, (128, 128), 1)
    to_z = jnp.where(ci == my_oz + (ri >> 1), 1.0, 0.0).astype(jnp.bfloat16)
    to_zface = jnp.where((ri == 127) & (ci == my_oz + 64), 1.0, 0.0) - jnp.where((ri == 0) & (ci == my_oz - 1), 1.0, 0.0)
    to_zface = to_zface.astype(jnp.bfloat16)
    same = (ri >> 3) == (ci >> 3)
    yr, yc = ri & 7, ci & 7
    to_y = jnp.where(same & (yr == my_oy + (yc >> 1)), 1.0, 0.0).astype(jnp.bfloat16)
    to_yface = jnp.where(same & (yc == 7) & (yr == my_oy + 4), 1.0, 0.0) - jnp.where(same & (yc == 0) & (yr == my_oy - 1), 1.0, 0.0)
    to_yface = to_yface.astype(jnp.bfloat16)
    placed = split_dot(wavg[0], to_z) + split_dot(wavg[1], to_zface)
    faces = split_dot(wavg[2], to_z)
    ends = split_dot(wx[...], to_z)
    middle = split_dot_left(to_y, placed) + split_dot_left(to_yface, faces)
    ends = split_dot_left(to_y, ends)
    vsend[pl.ds(1, 16)] = middle.reshape(16, 8, 128)
    vsend[0] = ends[0:8]
    vsend[17] = ends[8:16]

    back = [copy(vsend, vrecv.at[d], 6 + d, (r, peer(d))) for d in (1, 2, 3)]
    for one_copy in back:
        one_copy.start()
    vrecv[0] = jnp.zeros((18, 8, 128), F32)

    @pl.when(row_high)
    def _():
        down_copy.wait_recv()
        for f in range(2):
            for i in range(2):
                slab[f, NX + 2 + i, pl.ds(base_row, 8), :] = xhigh[f, i]

    @pl.when(jnp.logical_not(row_high))
    def _():
        for f in range(2):
            for i in range(2):
                slab[f, NX + 2 + i] = jnp.zeros((32, 128), F32)

    coarse_carry = coarse_start(62)
    for x in (62, 63):
        coarse_carry = coarse_plane(jnp.int32(x), coarse_carry)
    for x in range(54, NX):
        out_c[x] = base[x]
    for one_copy in back:
        one_copy.wait_recv()
    for k in range(3):
        def finish(i, carry, k=k):
            out_c[18 * k + i] = base[18 * k + i] + vrecv[slots[k], i]
            return carry

        lax.fori_loop(0, 18, finish, 0)
    for one_copy in (box_copy, patch_copy, start_copy) + tuple(back):
        one_copy.wait_send()

    @pl.when(has_side)
    def _():
        near_copy.wait_send()
        far_copy.wait_send()

    @pl.when(row_low)
    def _():
        down_copy.wait_send()

    @pl.when(row_high)
    def _():
        up_copy.wait_send()
        up_mate_copy.wait_send()


def per_device(*args):
    vmem = pl.BlockSpec(memory_space=pltpu.VMEM)

    def buf(*shape):
        return pltpu.VMEM(shape + (8, 128), F32)

    return pl.pallas_call(
        kernel,
        out_shape=(
            jax.ShapeDtypeStruct((64, 8, 128), F32),
            jax.ShapeDtypeStruct((32, 8, 128), F32),
        ),
        in_specs=[pl.BlockSpec(memory_space=pl.ANY)] * 9,
        out_specs=(vmem, vmem),
        scratch_shapes=[
            buf(NX),
            buf(3, NX),
            buf(3, NX),
            buf(32),
            buf(3, 32),
            buf(3, 32),
            pltpu.SMEM((1, args[6].shape[1]), jnp.int32),
            pltpu.SMEM((1, args[6].shape[1]), jnp.int32),
            pltpu.SMEM((1, args[6].shape[1]), jnp.int32),
            buf(4, NX),
            buf(4, NX),
            buf(2, 4, 2),
            buf(2, 2),
            buf(3 * NX // 4),
            buf(2, 3 * NX // 4),
            pltpu.VMEM((4, NX + 4, 32, 128), F32),
            buf(WX * PACK),
            buf(2, WX * PACK),
            buf(WX * TILES),
            buf(NX),
            buf(4, 5),
            buf(4, WX * TILES),
            pltpu.VMEM((4, 2, 40, 16, 128), F32),
            pltpu.VMEM((36, 16, 128), F32),
            buf(36),
            buf(18),
            buf(18),
            buf(18),
            pltpu.VMEM((3, 128, 128), F32),
            pltpu.VMEM((128, 128), F32),
            buf(18),
            buf(4, 18),
            pltpu.SemaphoreType.DMA((17,)),
            pltpu.SemaphoreType.DMA((11,)),
            pltpu.SemaphoreType.DMA((11,)),
            pltpu.SemaphoreType.REGULAR,
        ],
        compiler_params=pltpu.CompilerParams(
            collective_id=0, has_side_effects=True, vmem_limit_bytes=60 * 1024 * 1024
        ),
    )(*args)


def solution(mesh):
    in_specs = (
        P("row", "col", None),
        P(None, "row", "col", None),
        P(None, "row", "col", None),
        P("row", "col", None),
        P(None, "row", "col", None),
        P(None, "row", "col", None),
        P("row", None),
        P("row", None),
        P("row", None),
    )
    out_specs = (P("row", "col", None), P("row", "col", None))
    return jax.shard_map(
        per_device, mesh=mesh, in_specs=in_specs, out_specs=out_specs, check_vma=False
    )
```

```python
import jax
import jax.numpy as jnp
from jax import lax
from jax.experimental import pallas as pl
from jax.experimental.pallas import tpu as pltpu
from jax.sharding import PartitionSpec as P

MESH = pl.DeviceIdType.MESH
F32 = jnp.float32
NX = 64
WX = 22
TILES = 5
PACK = 3


def minmod(p, q):
    return jnp.maximum(jnp.minimum(p, q), 0.0) + jnp.minimum(jnp.maximum(p, q), 0.0)


def flux(sl, ml, sr, mr, w):
    q = 0.15 * w
    return w * jnp.where(w > 0, sl + (0.5 - q) * ml, sr - (0.5 + q) * mr)


def split_dot(values, matrix):
    high = values.astype(jnp.bfloat16)
    low = (values - high.astype(F32)).astype(jnp.bfloat16)
    return jnp.dot(high, matrix, preferred_element_type=F32) + jnp.dot(low, matrix, preferred_element_type=F32)


def split_dot_left(matrix, values):
    high = values.astype(jnp.bfloat16)
    low = (values - high.astype(F32)).astype(jnp.bfloat16)
    return jnp.dot(matrix, high, preferred_element_type=F32) + jnp.dot(matrix, low, preferred_element_type=F32)


def tile_iota(dim):
    return lax.broadcasted_iota(jnp.int32, (8, 128), dim)


def y_fluxes(s, b):
    d = [s[i + 1] - s[i] for i in range(4)]
    m = [minmod(d[i], d[i + 1]) for i in range(3)]
    low = flux(s[1], m[0], s[2], m[1], b[0] + b[1])
    high = flux(s[2], m[1], s[3], m[2], b[1] + b[2])
    return low, high


def kernel(
    cs_h, cv_h, cp_h, fs_h, fv_h, fp_h, shift_h, offy_h, offz_h,
    out_c, out_f,
    cv, cp, fs, fv, fp, shift, offy, offz,
    xlow, xhigh, ysend, yrecv, slab, msend, mbuf0, mbuf1, mbuf2, wide, base, masks,
    gh, fine, s1, s1z, fxs, ry, rz, wavg, wx, to_zs, to_ys, vsend, vrecv,
    load_sem, send_sem, recv_sem, ready,
):
    rows = lax.axis_size("row")
    cols = lax.axis_size("col")
    r = lax.axis_index("row")
    c = lax.axis_index("col")
    core = lax.rem(c, 2)
    j_me = lax.rem(c, 4)
    g0 = c - j_me
    sgn = 2 * core - 1
    mate = c + 1 - 2 * core
    chip = c // 2
    has_low = chip > 0
    has_high = chip < cols // 2 - 1
    row_low = r > 0
    row_high = r < rows - 1
    has_side = jnp.where(core == 0, has_low, has_high)

    base_row = pl.multiple_of(8 + 8 * core, 8)
    mate_row = pl.multiple_of(16 - 8 * core, 8)
    my_rows = pl.ds(base_row, 8)
    mate_rows = pl.ds(mate_row, 8)
    loads = [pltpu.make_async_copy(src, dst, load_sem.at[k]) for k, (src, dst) in enumerate(
        [(shift_h, shift), (offy_h, offy), (offz_h, offz), (cs_h, slab.at[0, pl.ds(2, NX), my_rows])]
        + [(cv_h.at[f], cv.at[f]) for f in range(3)] + [(cp_h.at[f], cp.at[f]) for f in range(3)]
        + [(fs_h, fs)] + [(fv_h.at[f], fv.at[f]) for f in range(3)] + [(fp_h.at[f], fp.at[f]) for f in range(3)]
    )]
    for load_copy in loads:
        load_copy.start()

    def peer(d):
        bit0, bit1 = lax.rem(j_me, 2), j_me // 2
        if d & 1:
            bit0 = 1 - bit0
        if d & 2:
            bit1 = 1 - bit1
        return g0 + 2 * bit1 + bit0

    near_low = g0 - 1
    near = c + sgn
    far = c + 2 * sgn

    barrier = pltpu.get_barrier_semaphore()

    def greet(*dev):
        pl.semaphore_signal(barrier, inc=1, device_id=dev, device_id_type=MESH)

    above = {1: core == 0, 2: j_me < 2, 3: j_me < 2}
    turned_up = (r == 0) & (c < 4)
    turned_dn = (r == 1) & (c < 4)

    for d in (1, 2, 3):
        @pl.when(jnp.logical_not(above[d]))
        def _(d=d):
            greet(r, peer(d))

    @pl.when((j_me < 2) & has_low)
    def _():
        greet(r, near_low)

    @pl.when((j_me == 0) & has_low)
    def _():
        greet(r, c - 2)

    @pl.when(row_high & jnp.logical_not(turned_up))
    def _():
        greet(r + 1, c)
        greet(r + 1, mate)

    @pl.when(turned_dn)
    def _():
        greet(r - 1, c)
        greet(r - 1, mate)

    greeters = 3 - j_me + jnp.where(has_high & (j_me >= 2), j_me - 1, 0)
    greeters = greeters + jnp.where(row_low & jnp.logical_not(turned_dn), 2, 0) + jnp.where(turned_up & row_high, 2, 0)

    @pl.when(greeters > 0)
    def _():
        pl.semaphore_wait(barrier, greeters)

    def answer(k, *dev):
        pl.semaphore_signal(ready.at[k], inc=1, device_id=dev, device_id_type=MESH)

    for d in (1, 2, 3):
        @pl.when(above[d])
        def _(d=d):
            answer(d, r, peer(d))

    @pl.when((j_me >= 2) & has_high)
    def _():
        answer(4, r, g0 + 4)

    @pl.when(row_low & jnp.logical_not(turned_dn))
    def _():
        answer(0, r - 1, c)
        answer(0, r - 1, mate)

    @pl.when(turned_up & row_high)
    def _():
        answer(5, r + 1, c)

    row = tile_iota(0)
    lane = tile_iota(1)
    l0 = lane == 0
    l127 = lane == 127

    for k in range(3):
        loads[k].wait()
    par = [j + shift[0, g0 + j] for j in range(4)]
    oyv = [offy[0, g0 + j] for j in range(4)]
    ozv = [offz[0, g0 + j] for j in range(4)]
    one = jnp.int32(1)
    zero = jnp.int32(0)
    rank = []
    for j in range(4):
        acc = zero
        for i in range(j):
            acc = acc + jnp.where(par[i] == par[j], one, zero)
        rank.append(acc)

    def pick(values, t):
        acc = zero
        for j in range(4):
            acc = acc + jnp.where(t == j, values[j], zero)
        return acc

    def half_plane(x):
        values = [0.75 * cv[f, x] - 0.25 * cp[f, x] for f in range(3)]
        for f in range(3):
            slab[f + 1, x + 2, my_rows, :] = values[f]
        return [slab[0, x + 2, my_rows, :]] + values

    def rows_at(value, at):
        return jnp.where(core == 0, pltpu.roll(value, at, 0) if at else value, pltpu.roll(value, (at + 2) % 8, 0))

    def half_coarse(h, carry):
        planes = [half_plane(4 * h + e) for e in range(4)]
        for t in range(2):
            tile = rows_at(planes[2 * t][0], 0)
            for k, value in ((2, planes[2 * t][2]), (4, planes[2 * t + 1][0]), (6, planes[2 * t + 1][2])):
                tile = jnp.where(row >= k, rows_at(value, k), tile)
            ysend[3 * h + t] = tile
        tile = None
        for e in range(4):
            for q in range(2):
                value, at = planes[e][2 * q + 1], 2 * e + q
                moved = jnp.where(core == 0, pltpu.roll(value, at, 0) if at else value, pltpu.roll(value, (at + 1) % 8, 0))
                tile = moved if tile is None else jnp.where(row >= at, moved, tile)
        ysend[3 * h + 2] = tile
        return carry

    for k in range(3, 10):
        loads[k].wait()
    lax.fori_loop(0, NX // 4, half_coarse, 0)

    def copy(src, dst, k, dev, kr=None):
        return pltpu.make_async_remote_copy(
            src_ref=src, dst_ref=dst, send_sem=send_sem.at[k], recv_sem=recv_sem.at[k if kr is None else kr],
            device_id=dev, device_id_type=MESH,
        )

    box = slab.at[:, pl.ds(2, NX), my_rows]
    box_copy = copy(box, box, 0, (r, mate))
    up_copy = copy(slab.at[:, pl.ds(NX, 2), my_rows], xlow.at[0], 1, (r + 1, c))
    up_mate_copy = copy(slab.at[:, pl.ds(NX, 2), my_rows], xlow.at[1], 2, (r + 1, mate))
    down_copy = copy(slab.at[pl.ds(0, 2), pl.ds(2, 2), my_rows], xhigh, 3, (r - 1, c))
    near_copy = copy(ysend, yrecv.at[1 - core], 4, (r, near), 5 - core)
    far_copy = copy(ysend, yrecv.at[1 - core], 5, (r, far), 5 - core)

    @pl.when((core == 1) & has_high)
    def _():
        near_copy.start()
        far_copy.start()

    @pl.when(core == 1)
    def _():
        pl.semaphore_wait(ready.at[1], 1)

    box_copy.start()

    @pl.when((j_me == 0) & has_low)
    def _():
        pl.semaphore_wait(ready.at[4], 2)
        near_copy.start()
        far_copy.start()

    @pl.when(j_me == 2)
    def _():
        pl.semaphore_wait(ready.at[3], 1)
        near_copy.start()
        pl.semaphore_wait(ready.at[2], 1)
        far_copy.start()

    @pl.when(turned_up & row_high)
    def _():
        up_copy.start()
        up_mate_copy.start()

    @pl.when(row_low & jnp.logical_not(turned_dn))
    def _():
        down_copy.start()

    def half_fine(x, carry):
        fine[0, 0, x + 4, pl.ds(4, 8), :] = fs[x]
        for f in range(3):
            fine[f + 1, 0, x + 4, pl.ds(4, 8), :] = 0.75 * fv[f, x] - 0.25 * fp[f, x]
        return carry

    for k in range(10, 17):
        loads[k].wait()
    lax.fori_loop(0, 32, half_fine, 0, unroll=4)

    slots = []
    for k in range(3):
        slot, oyk, ozk, valid = zero, zero, zero, zero
        for j in range(4):
            mine = jnp.where((par[j] == j_me) & (rank[j] == k), one, zero)
            dist0 = jnp.where(lax.rem(j_me, 2) == j % 2, zero, one)
            dist1 = jnp.where(j_me // 2 == j // 2, zero, one)
            slot = slot + mine * (dist0 + 2 * dist1)
            oyk = oyk + mine * oyv[j]
            ozk = ozk + mine * ozv[j]
            valid = valid + mine
        slots.append(slot)
        oyk = jnp.where(valid > 0, oyk, -100)
        iny = (row >= oyk) & (row < oyk + 4)
        inz = (lane >= ozk) & (lane < ozk + 64)
        masks[k, 0] = jnp.where((row == oyk - 1) & inz, 0.3, 0.0)
        masks[k, 1] = jnp.where((row == oyk + 4) & inz, 0.3, 0.0)
        masks[k, 2] = jnp.where((lane == ozk - 1) & iny, 0.3, 0.0)
        masks[k, 3] = jnp.where((lane == ozk + 64) & iny, 0.3, 0.0)
        masks[k, 4] = jnp.where(iny & inz, 1.0, 0.0)
    for q in range(5):
        masks[3, q] = jnp.zeros((8, 128), F32)


    @pl.when(has_low)
    def _():
        copy(ysend, yrecv.at[0], 4, (r, mate)).wait_recv()

    @pl.when(has_high)
    def _():
        copy(ysend, yrecv.at[1], 5, (r, mate)).wait_recv()

    for side, has in ((0, has_low), (1, has_high)):
        @pl.when(jnp.logical_not(has))
        def _(side=side):
            yrecv[side] = jnp.zeros((3 * NX // 4, 8, 128), F32)

    @pl.when(row_high & jnp.logical_not(turned_up))
    def _():
        pl.semaphore_wait(ready.at[0], 2)
        up_copy.start()
        up_mate_copy.start()

    def assemble(h, carry):
        for e in range(4):
            x = 4 * h + e
            for side, at in ((0, 6), (1, 24)):
                pair = 3 * h + e // 2
                slab[0, x + 2, pl.ds(at, 2), :] = yrecv[side, pair, pl.ds(4 * (e % 2), 2), :]
                slab[2, x + 2, pl.ds(at, 2), :] = yrecv[side, pair, pl.ds(4 * (e % 2) + 2, 2), :]
                alone = 7 if side == 0 else 24
                slab[1, x + 2, pl.ds(alone, 1), :] = yrecv[side, 3 * h + 2, pl.ds(2 * e, 1), :]
                slab[3, x + 2, pl.ds(alone, 1), :] = yrecv[side, 3 * h + 2, pl.ds(2 * e + 1, 1), :]
        return carry

    lax.fori_loop(0, NX // 4, assemble, 0)
    box_copy.wait_recv()

    def extractor(t):
        p = pick(par, t)
        first = 18 * pick(rank, t)
        r0 = 5 + 8 * lax.rem(p, 2) + pick(oyv, t)
        turn = 131 - pick(ozv, t)

        def plane(i, put):
            x = first + i

            def rolled(value, to):
                return pltpu.roll(value, lax.rem(turn + to, 128), 1)

            four = [slab[f, x, pl.ds(r0 + 1, 8), :] for f in range(4)]
            edge = slab[0, x, pl.ds(r0, 8), :]
            edge = jnp.where(row == 7, slab[0, x, pl.ds(r0 + 2, 8), :], edge)
            edge = jnp.where(row == 1, slab[2, x, pl.ds(r0 - 1, 8), :], edge)
            edge = jnp.where(row == 6, slab[2, x, pl.ds(r0 + 3, 8), :], edge)
            rest = rolled(edge, 0)
            for f in range(4):
                rest = jnp.where(lane >= 96 + 8 * f, rolled(four[f], 32 + 8 * f), rest)
            put(0, jnp.where(lane < 64, rolled(four[0], 0), rolled(four[1], 64)))
            put(1, jnp.where(lane < 64, rolled(four[2], 0), rolled(four[3], 64)))
            put(2, rest)

        return plane

    cross = extractor(lax.rem(j_me + 2, 4))
    mine = extractor(j_me)
    chunks = ((2, 12), (12, WX), (0, 2))
    mbufs = (mbuf0, mbuf1, mbuf2)

    def extract(k, plane, own):
        at, end = chunks[k]

        def step(i, carry):
            def put(q, value):
                if own:
                    mbufs[k][0, PACK * (i - at) + q] = value
                else:
                    msend[PACK * i + q] = value

            plane(i, put)
            return carry

        lax.fori_loop(at, end, step, 0, unroll=min(5, end - at))

    def chunk_copy(k):
        at, end = chunks[k]
        return copy(msend.at[pl.ds(PACK * at, PACK * (end - at))], mbufs[k].at[1], (6, 10, 11)[k], (r, peer(2)))

    patch_copies = [chunk_copy(k) for k in range(3)]
    extract(0, cross, False)

    @pl.when(j_me == 3)
    def _():
        pl.semaphore_wait(ready.at[2], 1)

    patch_copies[0].start()
    extract(1, cross, False)
    patch_copies[1].start()
    extract(0, mine, True)
    extract(1, mine, True)

    @pl.when(row_low)
    def _():
        up_copy.wait_recv()
        up_mate_copy.wait_recv()
        for f in range(4):
            for i in range(2):
                slab[f, i, pl.ds(base_row, 8), :] = xlow[0, f, i]
                slab[f, i, pl.ds(mate_row, 8), :] = xlow[1, f, i]

    @pl.when(jnp.logical_not(row_low))
    def _():
        for f in range(4):
            for i in range(2):
                slab[f, i] = jnp.zeros((32, 128), F32)

    extract(2, cross, False)
    patch_copies[2].start()
    extract(2, mine, True)

    def coarse_load(f, x, delta=0):
        return slab[f, x, pl.ds(base_row + delta, 8), :]

    def coarse_plane(x, carry):
        fxl, mx, sx, sn, ax = carry
        snn = coarse_load(0, x + 4)
        an = coarse_load(1, x + 3)
        mn = minmod(sn - sx, snn - sn)
        fxu = flux(sx, mx, sn, mn, ax + an)
        ys = [coarse_load(0, x + 2, d) for d in (-2, -1, 0, 1, 2)]
        yb = [coarse_load(2, x + 2, d) for d in (-1, 0, 1)]
        fyl, fyu = y_fluxes(ys, yb)
        vz = coarse_load(3, x + 2)
        up = jnp.where(l127, 0.0, pltpu.roll(sx, 127, 1))
        dn = jnp.where(l0, 0.0, pltpu.roll(sx, 1, 1))
        mz = minmod(sx - dn, up - sx)
        mu = jnp.where(l127, 0.0, pltpu.roll(mz, 127, 1))
        vu = jnp.where(l127, 0.0, pltpu.roll(vz, 127, 1))
        fzu = flux(sx, mz, up, mu, vz + vu)
        w0 = jnp.minimum(vz, 0.0)
        fzl = jnp.where(l0, w0 * (sx - (0.5 + 0.15 * w0) * mz), pltpu.roll(fzu, 1, 1))
        new = sx - 0.3 * ((fxu - fxl) + (fyu - fyl) + (fzu - fzl))
        k = x // 18
        i = x - 18 * k
        mid = jnp.where((i >= 1) & (i <= 16), 1.0, 0.0).astype(F32)
        lowx = jnp.where(i == 0, 0.3, 0.0).astype(F32)
        highx = jnp.where(i == 17, 0.3, 0.0).astype(F32)
        cov = masks[k, 4]
        new = new + mid * (masks[k, 0] * fyu - masks[k, 1] * fyl + masks[k, 2] * fzu - masks[k, 3] * fzl)
        new = new + cov * (lowx * fxu - highx * fxl)
        base[x] = jnp.where(cov * mid > 0, 0.0, new)
        return fxu, mn, sn, snn, an

    def coarse_group(h, carry):
        for e in range(6):
            carry = coarse_plane(6 * h + e, carry)
        return carry

    def coarse_start(x):
        p0, p1, p2, p3 = [coarse_load(0, x + i) for i in range(4)]
        v1, v2 = coarse_load(1, x + 1), coarse_load(1, x + 2)
        m1, m2 = minmod(p1 - p0, p2 - p1), minmod(p2 - p1, p3 - p2)
        return flux(p1, m1, p2, m2, v1 + v2), m2, p2, p3, v2

    lax.fori_loop(0, 5, coarse_group, coarse_start(0))

    @pl.when(turned_dn)
    def _():
        pl.semaphore_wait(ready.at[5], 1)
        down_copy.start()

    my_par = pick(par, j_me)
    my_oy = pick(oyv, j_me)
    my_oz = pick(ozv, j_me)
    sel = jnp.where(my_par // 2 == j_me // 2, zero, one)
    zi = lax.broadcasted_iota(jnp.int32, (128, 512), 0)
    qi = lax.broadcasted_iota(jnp.int32, (128, 512), 1)
    lq = qi & 127
    cell0 = my_oz + (lq >> 1)
    cell1 = jnp.where(lq < 4, my_oz + 64 + (lq >> 1), jnp.where(lq >= 124, my_oz + ((lq - 128) >> 1), -1000))
    cell = jnp.where((qi & 128) == 0, cell0, cell1)
    slope = jnp.where(qi >= 256, jnp.where((qi & 1) == 0, -0.125, 0.125), 0.0)
    zi = jnp.where((zi < 70) & (zi + my_oz >= 3) & (zi + my_oz < 131), zi + my_oz - 3, -5000)
    zmat = jnp.where(zi == cell, 1.0, 0.0) + jnp.where(zi == cell + 1, slope, 0.0) - jnp.where(zi == cell - 1, slope, 0.0)
    zmat = zmat.astype(jnp.bfloat16)

    ri = lax.broadcasted_iota(jnp.int32, (128, 128), 0)
    ci = lax.broadcasted_iota(jnp.int32, (128, 128), 1)
    to_zs[0] = jnp.where(ci == my_oz + (ri >> 1), 1.0, 0.0).astype(jnp.bfloat16)
    to_zface = jnp.where((ri == 127) & (ci == my_oz + 64), 1.0, 0.0) - jnp.where((ri == 0) & (ci == my_oz - 1), 1.0, 0.0)
    to_zs[1] = to_zface.astype(jnp.bfloat16)
    same = (ri >> 3) == (ci >> 3)
    yr, yc = ri & 7, ci & 7
    to_ys[0] = jnp.where(same & (yr == my_oy + (yc >> 1)), 1.0, 0.0).astype(jnp.bfloat16)
    to_yface = jnp.where(same & (yc == 7) & (yr == my_oy + 4), 1.0, 0.0) - jnp.where(same & (yc == 0) & (yr == my_oy - 1), 1.0, 0.0)
    to_ys[1] = to_yface.astype(jnp.bfloat16)

    def unpack_chunk(k):
        at, end = chunks[k]
        patch_copies[k].wait_recv()

        def unpack(i, carry):
            first, second, rest = [mbufs[k][sel, PACK * (i - at) + q] for q in range(PACK)]
            for f, value in enumerate((first, pltpu.roll(first, 64, 1), second, pltpu.roll(second, 64, 1))):
                wide[TILES * i + f] = jnp.where(lane < 64, value, pltpu.roll(rest, 96 - 8 * f, 1))
            wide[TILES * i + 4] = rest
            return carry

        lax.fori_loop(at, end, unpack, 0, unroll=min(5, end - at))
        part, size = pl.ds(TILES * at, TILES * (end - at)), TILES * (end - at)
        res = split_dot(wide[part].reshape(size * 8, 128), zmat)
        for q in range(4):
            gh[q, part] = res[:, 128 * q:128 * (q + 1)].reshape(size, 8, 128)

    def refine_plane(i, full):
        for lt in range(2):
            edge = gh[lt, TILES * i + 4]
            for f in range(4):
                g = gh[lt, TILES * i + f]
                sx = 0.125 * (gh[lt, TILES * (i + 1) + f] - gh[lt, TILES * (i - 1) + f])
                lo = pltpu.roll(g, 1, 0)
                hi = pltpu.roll(g, 7, 0)
                if f == 0:
                    lo = jnp.where(row == 0, edge, lo)
                    hi = jnp.where(row == 7, edge, hi)
                if f == 2:
                    lo = jnp.where(row == 0, pltpu.roll(edge, 7, 0), lo)
                    hi = jnp.where(row == 7, pltpu.roll(edge, 1, 0), hi)
                sy = 0.125 * (hi - lo)
                ctr = gh[2 + lt, TILES * i + f]
                for e in range(2):
                    cx = ctr + sx if e else ctr - sx
                    for ey in range(2):
                        value = cx + sy if ey else cx - sy
                        xf = 2 * (i - 1) + e
                        if full or lt == 1:
                            fine[f, lt, xf, pl.ds(ey, 8, stride=2), :] = value
                        else:
                            fine[f, lt, xf, pl.ds(ey, 2, stride=2), :] = value[0:2]
                            fine[f, lt, xf, pl.ds(12 + ey, 2, stride=2), :] = value[6:8]

    def refine(at, end, full):
        def step(i, carry):
            refine_plane(i, full)
            return carry

        lax.fori_loop(at, end, step, 0)

    def zup(t0, t1):
        a0, a1 = pltpu.roll(t0, 127, 1), pltpu.roll(t1, 127, 1)
        return jnp.where(l127, a1, a0), jnp.where(l127, a0, a1)

    def zdn(t0, t1):
        a0, a1 = pltpu.roll(t0, 1, 1), pltpu.roll(t1, 1, 1)
        return jnp.where(l0, a1, a0), jnp.where(l0, a0, a1)

    def z_fluxes(t0, t1, w0, w1):
        u0, u1 = zup(t0, t1)
        d0, d1 = zdn(t0, t1)
        n0, n1 = minmod(t0 - d0, u0 - t0), minmod(t1 - d1, u1 - t1)
        nu0, nu1 = zup(n0, n1)
        wu0, wu1 = zup(w0, w1)
        h0, h1 = flux(t0, n0, u0, nu0, w0 + wu0), flux(t1, n1, u1, nu1, w1 + wu1)
        b0, b1 = zdn(h0, h1)
        return b0, h0, b1, h1

    def load(block, f, x, d=0):
        if block == 0:
            return fine[f, 0, x, pl.ds(4 + d, 8), :]
        if block == 1:
            return fine[f, 1, x, pl.ds(4 + d, 8), :]
        return jnp.where(row < 4, fine[f, 0, x, pl.ds(2 + d, 8), :], fine[f, 0, x, pl.ds(6 + d, 8), :])

    def load_pad(f, x):
        return jnp.where(row < 4, fine[f, 1, x, pl.ds(2, 8), :], fine[f, 1, x, pl.ds(6, 8), :])

    def x_start(block, x):
        a0, a1, a2, a3 = [load(block, 0, x + d) for d in (-2, -1, 0, 1)]
        w0, w1 = load(block, 1, x - 1), load(block, 1, x)
        n1, n2 = minmod(a1 - a0, a2 - a1), minmod(a2 - a1, a3 - a2)
        return flux(a1, n1, a2, n2, w0 + w1), n2, a2, a3, w1

    def x_next(block, x, carry):
        fxl, mx, sx, sn, ax = carry
        snn = load(block, 0, x + 2)
        an = load(block, 1, x + 1)
        mn = minmod(sn - sx, snn - sn)
        fxu = flux(sx, mx, sn, mn, ax + an)
        return fxl, fxu, (fxu, mn, sn, snn, an)

    def first_plane(x, carries):
        out, xs, ys = [], [], []
        for block in range(3):
            fxl, fxu, nxt = x_next(block, x, carries[block])
            out.append(nxt)
            xs.append((fxl, fxu))
            ys.append(y_fluxes([load(block, 0, x, d) for d in (-2, -1, 0, 1, 2)], [load(block, 2, x, d) for d in (-1, 0, 1)]))
        c0, c1, c2 = carries[0][2], carries[1][2], carries[2][2]
        zl0, zu0, zl1, zu1 = z_fluxes(c0, c1, load(0, 3, x), load(1, 3, x))
        zl2, zu2, _, _ = z_fluxes(c2, load_pad(0, x), load(2, 3, x), load_pad(3, x))
        news = []
        for sc, (xl, xu), (yl, yu), (zl, zu) in zip((c0, c1, c2), xs, ys, ((zl0, zu0), (zl1, zu1), (zl2, zu2))):
            news.append(sc - 0.3 * ((xu - xl) + (yu - yl) + (zu - zl)))
        s1[x - 2, pl.ds(2, 8), :] = news[0]
        s1[x - 2, pl.ds(0, 2), :] = news[2][0:2]
        s1[x - 2, pl.ds(10, 2), :] = news[2][6:8]
        s1z[x - 2] = news[1]
        reg_y = jnp.where(row == 0, ys[0][0], jnp.where(row == 7, ys[0][1], 0.0))
        reg_z = jnp.where(l0, zl0, jnp.where(l127, zu0, 0.0))
        return tuple(out), reg_y, reg_z, xs[0][1]

    def first_pair(h, carries):
        carries, ya, za, _ = first_plane(2 + 2 * h, carries)
        carries, yb, zb, fx = first_plane(3 + 2 * h, carries)
        ry[h] = ya + yb
        rz[h] = za + zb
        fxs[h] = fx
        return carries

    def first_group(h, carries):
        for e in range(2):
            carries = first_pair(2 * h + e, carries)
        return carries

    unpack_chunk(0)
    refine(3, 11, False)
    carries = lax.fori_loop(1, 4, first_group, tuple(x_start(block, 6) for block in range(3)))
    unpack_chunk(1)
    refine(11, 19, False)
    refine(19, 21, True)
    lax.fori_loop(4, 9, first_group, carries)
    unpack_chunk(2)
    refine(1, 3, True)
    first_group(0, tuple(x_start(block, 2) for block in range(3)))

    def second_load(x, d=0):
        return s1[x + 2, pl.ds(2 + d, 8), :]

    def second_plane(x, carry):
        fxl, mx, sx, sn, ax = carry
        snn = second_load(x + 2)
        an = load(0, 1, x + 5)
        mn = minmod(sn - sx, snn - sn)
        fxu = flux(sx, mx, sn, mn, ax + an)
        yl, yu = y_fluxes([second_load(x, d) for d in (-2, -1, 0, 1, 2)], [load(0, 2, x + 4, d) for d in (-1, 0, 1)])
        zl, zu, _, _ = z_fluxes(sx, s1z[x + 2], load(0, 3, x + 4), load(1, 3, x + 4))
        new = sx - 0.3 * ((fxu - fxl) + (yu - yl) + (zu - zl))
        out_f[x] = new
        reg_y = jnp.where(row == 0, yl, jnp.where(row == 7, yu, 0.0))
        reg_z = jnp.where(l0, zl, jnp.where(l127, zu, 0.0))
        return (fxu, mn, sn, snn, an), new, reg_y, reg_z

    def second_pair(h, carry):
        carry, na, ya, za = second_plane(2 * h, carry)
        carry, nb, yb, zb = second_plane(2 * h + 1, carry)
        at = pl.ds(pl.multiple_of(8 * h, 8), 8)
        wavg[0, at, :] = 0.125 * (na + nb)
        wavg[1, at, :] = 0.0375 * (rz[h + 1] + (za + zb))
        wavg[2, at, :] = 0.0375 * (ry[h + 1] + (ya + yb))
        return carry

    q0, q1, q2, q3 = [second_load(i) for i in (-2, -1, 0, 1)]
    u1, u2 = load(0, 1, 3), load(0, 1, 4)
    k1, k2 = minmod(q1 - q0, q2 - q1), minmod(q2 - q1, q3 - q2)
    x_low = flux(q1, k1, q2, k2, u1 + u2)
    def second_group(h, carry):
        for e in range(4):
            carry = second_pair(4 * h + e, carry)
        return carry

    def place(at, count):
        part = pl.ds(8 * at, 8 * count)
        to_y, to_yface = to_ys[0, 0:8 * count, 0:8 * count], to_ys[1, 0:8 * count, 0:8 * count]
        placed = split_dot(wavg[0, part], to_zs[0]) + split_dot(wavg[1, part], to_zs[1])
        faces = split_dot(wavg[2, part], to_zs[0])
        middle = split_dot_left(to_y, placed) + split_dot_left(to_yface, faces)
        vsend[pl.ds(at, count)] = middle.reshape(count, 8, 128)

    @pl.when(j_me == 3)
    def _():
        pl.semaphore_wait(ready.at[3], 1)

    def back_copy(d, k):
        part = pl.ds(8 * k, 8 + 2 * k)
        return copy(vsend.at[part], vrecv.at[d, part], 6 + d if k == 0 else 11 + d, (r, peer(d)))

    back = [[back_copy(d, k) for d in (2, 3, 1)] for k in range(2)]
    carry = lax.fori_loop(0, 2, second_group, (x_low, k2, q2, q3, u2))
    place(0, 8)
    for one_copy in back[0]:
        one_copy.start()
    x_high = lax.fori_loop(2, 4, second_group, carry)[0]
    wx[pl.ds(0, 8), :] = -0.0375 * (fxs[0] + x_low)
    wx[pl.ds(8, 8), :] = 0.0375 * (fxs[16] + x_high)
    place(8, 8)
    vsend[pl.ds(16, 2)] = split_dot_left(to_ys[0, 0:16, 0:16], split_dot(wx[...], to_zs[0])).reshape(2, 8, 128)
    for one_copy in back[1]:
        one_copy.start()
    back = back[0] + back[1]
    vrecv[0] = jnp.zeros((18, 8, 128), F32)

    coarse_carry = lax.fori_loop(5, 10, coarse_group, coarse_start(30))
    for x in (60, 61):
        coarse_carry = coarse_plane(jnp.int32(x), coarse_carry)

    @pl.when(row_high)
    def _():
        down_copy.wait_recv()
        for f in range(2):
            for i in range(2):
                slab[f, NX + 2 + i, pl.ds(base_row, 8), :] = xhigh[f, i]

    @pl.when(jnp.logical_not(row_high))
    def _():
        for f in range(2):
            for i in range(2):
                slab[f, NX + 2 + i] = jnp.zeros((32, 128), F32)

    for x in (62, 63):
        coarse_carry = coarse_plane(jnp.int32(x), coarse_carry)
    for x in range(54, NX):
        out_c[x] = base[x]
    for one_copy in back:
        one_copy.wait_recv()
    for k in range(3):
        def finish(i, carry, k=k):
            out_c[18 * k + 1 + i] = base[18 * k + 1 + i] + vrecv[slots[k], i]
            return carry

        lax.fori_loop(0, 16, finish, 0, unroll=8)
        for x, i in ((18 * k, 16), (18 * k + 17, 17)):
            out_c[x] = base[x] + vrecv[slots[k], i]
    for one_copy in [box_copy] + patch_copies + back:
        one_copy.wait_send()

    @pl.when(has_side)
    def _():
        near_copy.wait_send()
        far_copy.wait_send()

    @pl.when(row_low)
    def _():
        down_copy.wait_send()

    @pl.when(row_high)
    def _():
        up_copy.wait_send()
        up_mate_copy.wait_send()


def per_device(*args):
    vmem = pl.BlockSpec(memory_space=pltpu.VMEM)

    def buf(*shape):
        return pltpu.VMEM(shape + (8, 128), F32)

    return pl.pallas_call(
        kernel,
        out_shape=(
            jax.ShapeDtypeStruct((64, 8, 128), F32),
            jax.ShapeDtypeStruct((32, 8, 128), F32),
        ),
        in_specs=[pl.BlockSpec(memory_space=pl.ANY)] * 9,
        out_specs=(vmem, vmem),
        scratch_shapes=[
            buf(3, NX),
            buf(3, NX),
            buf(32),
            buf(3, 32),
            buf(3, 32),
            pltpu.SMEM((1, args[6].shape[1]), jnp.int32),
            pltpu.SMEM((1, args[6].shape[1]), jnp.int32),
            pltpu.SMEM((1, args[6].shape[1]), jnp.int32),
            buf(2, 4, 2),
            buf(2, 2),
            buf(3 * NX // 4),
            buf(2, 3 * NX // 4),
            pltpu.VMEM((4, NX + 4, 32, 128), F32),
            buf(WX * PACK),
            buf(2, 10 * PACK),
            buf(2, 10 * PACK),
            buf(2, 2 * PACK),
            buf(WX * TILES),
            buf(NX),
            buf(4, 5),
            buf(4, WX * TILES),
            pltpu.VMEM((4, 2, 40, 16, 128), F32),
            pltpu.VMEM((36, 16, 128), F32),
            buf(36),
            buf(18),
            buf(18),
            buf(18),
            pltpu.VMEM((3, 128, 128), F32),
            pltpu.VMEM((16, 128), F32),
            pltpu.VMEM((2, 128, 128), jnp.bfloat16),
            pltpu.VMEM((2, 128, 128), jnp.bfloat16),
            buf(18),
            buf(4, 18),
            pltpu.SemaphoreType.DMA((17,)),
            pltpu.SemaphoreType.DMA((15,)),
            pltpu.SemaphoreType.DMA((15,)),
            pltpu.SemaphoreType.REGULAR((6,)),
        ],
        compiler_params=pltpu.CompilerParams(
            collective_id=0, has_side_effects=True, vmem_limit_bytes=60 * 1024 * 1024
        ),
    )(*args)


def solution(mesh):
    in_specs = (
        P("row", "col", None),
        P(None, "row", "col", None),
        P(None, "row", "col", None),
        P("row", "col", None),
        P(None, "row", "col", None),
        P(None, "row", "col", None),
        P("row", None),
        P("row", None),
        P("row", None),
    )
    out_specs = (P("row", "col", None), P("row", "col", None))
    return jax.shard_map(
        per_device, mesh=mesh, in_specs=in_specs, out_specs=out_specs, check_vma=False
    )
```

```python
import jax
import jax.numpy as jnp
from jax import lax
from jax.experimental import pallas as pl
from jax.experimental.pallas import tpu as pltpu
from jax.sharding import PartitionSpec as P

MESH = pl.DeviceIdType.MESH
F32 = jnp.float32
NX = 64
WX = 22
TILES = 5
PACK = 5


def minmod(p, q):
    return jnp.maximum(jnp.minimum(p, q), 0.0) + jnp.minimum(jnp.maximum(p, q), 0.0)


def flux(sl, ml, sr, mr, w):
    q = 0.15 * w
    return w * jnp.where(w > 0, sl + (0.5 - q) * ml, sr - (0.5 + q) * mr)


def split_dot(values, matrix):
    high = values.astype(jnp.bfloat16)
    low = (values - high.astype(F32)).astype(jnp.bfloat16)
    return jnp.dot(high, matrix, preferred_element_type=F32) + jnp.dot(low, matrix, preferred_element_type=F32)


def split_dot_left(matrix, values):
    high = values.astype(jnp.bfloat16)
    low = (values - high.astype(F32)).astype(jnp.bfloat16)
    return jnp.dot(matrix, high, preferred_element_type=F32) + jnp.dot(matrix, low, preferred_element_type=F32)


def tile_iota(dim):
    return lax.broadcasted_iota(jnp.int32, (8, 128), dim)


def y_fluxes(s, b):
    d = [s[i + 1] - s[i] for i in range(4)]
    m = [minmod(d[i], d[i + 1]) for i in range(3)]
    low = flux(s[1], m[0], s[2], m[1], b[0] + b[1])
    high = flux(s[2], m[1], s[3], m[2], b[1] + b[2])
    return low, high


def kernel(
    cs_h, cv_h, cp_h, fs_h, fv_h, fp_h, shift_h, offy_h, offz_h,
    out_c, out_f,
    cv, cp, fs, fv, fp, shift, offy, offz,
    xlow, xhigh, ysend, yrecv, slab, msend, mbuf0, mbuf1, mbuf2, wide, base, masks,
    gh, fine, s1, s1z, fxs, ry, rz, wavg, wx, to_zs, to_ys, vsend, vrecv,
    load_sem, send_sem, recv_sem, ready,
):
    rows = lax.axis_size("row")
    cols = lax.axis_size("col")
    r = lax.axis_index("row")
    c = lax.axis_index("col")
    core = lax.rem(c, 2)
    j_me = lax.rem(c, 4)
    g0 = c - j_me
    sgn = 2 * core - 1
    mate = c + 1 - 2 * core
    chip = c // 2
    has_low = chip > 0
    has_high = chip < cols // 2 - 1
    row_low = r > 0
    row_high = r < rows - 1
    has_side = jnp.where(core == 0, has_low, has_high)

    base_row = pl.multiple_of(8 + 8 * core, 8)
    mate_row = pl.multiple_of(16 - 8 * core, 8)
    my_rows = pl.ds(base_row, 8)
    mate_rows = pl.ds(mate_row, 8)
    half = NX // 2
    pairs = [(shift_h, shift), (offy_h, offy), (offz_h, offz)]
    for h in range(2):
        xs = pl.ds(half * h, half)
        pairs.append((cs_h.at[xs], slab.at[0, pl.ds(2 + half * h, half), my_rows]))
        pairs += [(cv_h.at[f, xs], cv.at[f, xs]) for f in range(3)] + [(cp_h.at[f, xs], cp.at[f, xs]) for f in range(3)]
    pairs += [(fs_h, fs)] + [(fv_h.at[f], fv.at[f]) for f in range(3)] + [(fp_h.at[f], fp.at[f]) for f in range(3)]
    loads = [pltpu.make_async_copy(src, dst, load_sem.at[k]) for k, (src, dst) in enumerate(pairs)]
    for load_copy in loads:
        load_copy.start()

    def peer(d):
        bit0, bit1 = lax.rem(j_me, 2), j_me // 2
        if d & 1:
            bit0 = 1 - bit0
        if d & 2:
            bit1 = 1 - bit1
        return g0 + 2 * bit1 + bit0

    near = c + sgn

    barrier = pltpu.get_barrier_semaphore()

    def greet(*dev):
        pl.semaphore_signal(barrier, inc=1, device_id=dev, device_id_type=MESH)

    above = {1: core == 0, 2: j_me < 2, 3: j_me < 2}
    turned_up = (r == 0) & (c < 4)
    turned_dn = (r == 1) & (c < 4)

    for d in (1, 2, 3):
        @pl.when(jnp.logical_not(above[d]))
        def _(d=d):
            greet(r, peer(d))

    @pl.when((j_me == 0) & has_low)
    def _():
        greet(r, c - 1)

    @pl.when(row_high & jnp.logical_not(turned_up))
    def _():
        greet(r + 1, c)
        greet(r + 1, mate)

    @pl.when(turned_dn)
    def _():
        greet(r - 1, c)
        greet(r - 1, mate)

    greeters = 3 - j_me + jnp.where(has_high & (j_me == 3), 1, 0)
    greeters = greeters + jnp.where(row_low & jnp.logical_not(turned_dn), 2, 0) + jnp.where(turned_up & row_high, 2, 0)

    @pl.when(greeters > 0)
    def _():
        pl.semaphore_wait(barrier, greeters)

    def answer(k, *dev):
        pl.semaphore_signal(ready.at[k], inc=1, device_id=dev, device_id_type=MESH)

    for d in (1, 2, 3):
        @pl.when(above[d])
        def _(d=d):
            answer(d, r, peer(d))

    @pl.when((j_me == 3) & has_high)
    def _():
        answer(4, r, c + 1)

    @pl.when(row_low & jnp.logical_not(turned_dn))
    def _():
        answer(0, r - 1, c)
        answer(0, r - 1, mate)

    @pl.when(turned_up & row_high)
    def _():
        answer(5, r + 1, c)

    row = tile_iota(0)
    lane = tile_iota(1)
    l0 = lane == 0
    l127 = lane == 127

    for k in range(3):
        loads[k].wait()
    par = [j + shift[0, g0 + j] for j in range(4)]
    oyv = [offy[0, g0 + j] for j in range(4)]
    ozv = [offz[0, g0 + j] for j in range(4)]
    one = jnp.int32(1)
    zero = jnp.int32(0)
    rank = []
    for j in range(4):
        acc = zero
        for i in range(j):
            acc = acc + jnp.where(par[i] == par[j], one, zero)
        rank.append(acc)

    def pick(values, t):
        acc = zero
        for j in range(4):
            acc = acc + jnp.where(t == j, values[j], zero)
        return acc

    def half_plane(x):
        values = [0.75 * cv[f, x] - 0.25 * cp[f, x] for f in range(3)]
        for f in range(3):
            slab[f + 1, x + 2, my_rows, :] = values[f]
        return [slab[0, x + 2, my_rows, :]] + values

    def rows_at(value, at):
        return jnp.where(core == 0, pltpu.roll(value, at, 0) if at else value, pltpu.roll(value, (at + 2) % 8, 0))

    def half_coarse(h, carry):
        planes = [half_plane(4 * h + e) for e in range(4)]
        for t in range(2):
            tile = rows_at(planes[2 * t][0], 0)
            for k, value in ((2, planes[2 * t][2]), (4, planes[2 * t + 1][0]), (6, planes[2 * t + 1][2])):
                tile = jnp.where(row >= k, rows_at(value, k), tile)
            ysend[3 * h + t] = tile
        tile = None
        for e in range(4):
            for q in range(2):
                value, at = planes[e][2 * q + 1], 2 * e + q
                moved = jnp.where(core == 0, pltpu.roll(value, at, 0) if at else value, pltpu.roll(value, (at + 1) % 8, 0))
                tile = moved if tile is None else jnp.where(row >= at, moved, tile)
        ysend[3 * h + 2] = tile
        return carry

    def copy(src, dst, k, dev, kr=None):
        return pltpu.make_async_remote_copy(
            src_ref=src, dst_ref=dst, send_sem=send_sem.at[k], recv_sem=recv_sem.at[k if kr is None else kr],
            device_id=dev, device_id_type=MESH,
        )

    boxes = [slab.at[:, pl.ds(2 + half * h, half), my_rows] for h in range(2)]
    box_copies = [copy(boxes[h], boxes[h], 15 * h, (r, mate)) for h in range(2)]
    for k in range(3, 10):
        loads[k].wait()
    lax.fori_loop(0, NX // 8, half_coarse, 0)

    @pl.when(core == 0)
    def _():
        box_copies[0].start()

    for k in range(10, 17):
        loads[k].wait()
    lax.fori_loop(NX // 8, NX // 4, half_coarse, 0)

    up_copy = copy(slab.at[:, pl.ds(NX, 2), my_rows], xlow.at[0], 1, (r + 1, c))
    up_mate_copy = copy(slab.at[:, pl.ds(NX, 2), my_rows], xlow.at[1], 2, (r + 1, mate))
    down_copy = copy(slab.at[pl.ds(0, 2), pl.ds(2, 2), my_rows], xhigh, 3, (r - 1, c))
    near_copy = copy(ysend, yrecv.at[1 - core], 4, (r, near), 5 - core)
    hand_copy = copy(yrecv.at[core], yrecv.at[core], 5, (r, mate), 4 + core)

    @pl.when((core == 1) & has_high)
    def _():
        near_copy.start()

    @pl.when(core == 1)
    def _():
        pl.semaphore_wait(ready.at[1], 1)
        box_copies[0].start()

    box_copies[1].start()

    @pl.when((j_me == 0) & has_low)
    def _():
        pl.semaphore_wait(ready.at[4], 1)
        near_copy.start()

    @pl.when(j_me == 2)
    def _():
        pl.semaphore_wait(ready.at[3], 1)
        near_copy.start()

    @pl.when(turned_up & row_high)
    def _():
        up_copy.start()
        up_mate_copy.start()

    @pl.when(row_low & jnp.logical_not(turned_dn))
    def _():
        down_copy.start()

    def half_fine(x, carry):
        fine[0, 0, x + 4, pl.ds(4, 8), :] = fs[x]
        for f in range(3):
            fine[f + 1, 0, x + 4, pl.ds(4, 8), :] = 0.75 * fv[f, x] - 0.25 * fp[f, x]
        return carry

    for k in range(17, 24):
        loads[k].wait()
    lax.fori_loop(0, 32, half_fine, 0, unroll=4)

    slots = []
    for k in range(3):
        slot, oyk, ozk, valid = zero, zero, zero, zero
        for j in range(4):
            mine = jnp.where((par[j] == j_me) & (rank[j] == k), one, zero)
            dist0 = jnp.where(lax.rem(j_me, 2) == j % 2, zero, one)
            dist1 = jnp.where(j_me // 2 == j // 2, zero, one)
            slot = slot + mine * (dist0 + 2 * dist1)
            oyk = oyk + mine * oyv[j]
            ozk = ozk + mine * ozv[j]
            valid = valid + mine
        slots.append(slot)
        oyk = jnp.where(valid > 0, oyk, -100)
        iny = (row >= oyk) & (row < oyk + 4)
        inz = (lane >= ozk) & (lane < ozk + 64)
        masks[k, 0] = jnp.where((row == oyk - 1) & inz, 0.3, 0.0)
        masks[k, 1] = jnp.where((row == oyk + 4) & inz, 0.3, 0.0)
        masks[k, 2] = jnp.where((lane == ozk - 1) & iny, 0.3, 0.0)
        masks[k, 3] = jnp.where((lane == ozk + 64) & iny, 0.3, 0.0)
        masks[k, 4] = jnp.where(iny & inz, 1.0, 0.0)
    for q in range(5):
        masks[3, q] = jnp.zeros((8, 128), F32)


    @pl.when(has_side)
    def _():
        copy(ysend, yrecv.at[core], 4, (r, near), 4 + core).wait_recv()
        hand_copy.start()

    @pl.when(jnp.where(core == 0, has_high, has_low))
    def _():
        copy(yrecv.at[1 - core], yrecv.at[1 - core], 5, (r, mate), 5 - core).wait_recv()

    for side, has in ((0, has_low), (1, has_high)):
        @pl.when(jnp.logical_not(has))
        def _(side=side):
            yrecv[side] = jnp.zeros((3 * NX // 4, 8, 128), F32)

    @pl.when(row_high & jnp.logical_not(turned_up))
    def _():
        pl.semaphore_wait(ready.at[0], 2)
        up_copy.start()
        up_mate_copy.start()

    def assemble(h, carry):
        for e in range(4):
            x = 4 * h + e
            for side, at in ((0, 6), (1, 24)):
                pair = 3 * h + e // 2
                slab[0, x + 2, pl.ds(at, 2), :] = yrecv[side, pair, pl.ds(4 * (e % 2), 2), :]
                slab[2, x + 2, pl.ds(at, 2), :] = yrecv[side, pair, pl.ds(4 * (e % 2) + 2, 2), :]
                alone = 7 if side == 0 else 24
                slab[1, x + 2, pl.ds(alone, 1), :] = yrecv[side, 3 * h + 2, pl.ds(2 * e, 1), :]
                slab[3, x + 2, pl.ds(alone, 1), :] = yrecv[side, 3 * h + 2, pl.ds(2 * e + 1, 1), :]
        return carry

    lax.fori_loop(0, NX // 4, assemble, 0)
    for one_copy in box_copies:
        one_copy.wait_recv()

    def extractor(t):
        p = pick(par, t)
        first = 18 * pick(rank, t)
        r0 = 5 + 8 * lax.rem(p, 2) + pick(oyv, t)
        turn = 131 - pick(ozv, t)

        def pair(h, put):
            def rolled(value, to):
                return pltpu.roll(value, lax.rem(turn + to, 128), 1)

            rest = []
            for e in range(2):
                x = first + 2 * h + e
                four = [slab[f, x, pl.ds(r0 + 1, 8), :] for f in range(4)]
                edge = slab[0, x, pl.ds(r0, 8), :]
                edge = jnp.where(row == 7, slab[0, x, pl.ds(r0 + 2, 8), :], edge)
                edge = jnp.where(row == 1, slab[2, x, pl.ds(r0 - 1, 8), :], edge)
                edge = jnp.where(row == 6, slab[2, x, pl.ds(r0 + 3, 8), :], edge)
                rest.append((rolled(edge, 0), four))
                put(2 * e, jnp.where(lane < 64, rolled(four[0], 0), rolled(four[1], 64)))
                put(2 * e + 1, jnp.where(lane < 64, rolled(four[2], 0), rolled(four[3], 64)))
            both = jnp.where((row < 2) | (row >= 6), rest[0][0], jnp.where(row < 4, pltpu.roll(rest[1][0], 2, 0), pltpu.roll(rest[1][0], 6, 0)))
            for e in range(2):
                for f in range(4):
                    at = 72 + 24 * e + 6 * f
                    both = jnp.where(lane >= at, rolled(rest[e][1][f], at - 64), both)
            put(4, both)

        return pair

    cross = extractor(lax.rem(j_me + 2, 4))
    mine = extractor(j_me)
    chunks = ((2, 14), (14, WX), (0, 2))
    mbufs = (mbuf0, mbuf1, mbuf2)

    def extract(k, pair, own):
        at, end = chunks[k][0] // 2, chunks[k][1] // 2

        def step(h, carry):
            def put(q, value):
                if own:
                    mbufs[k][0, PACK * (h - at) + q] = value
                else:
                    msend[PACK * h + q] = value

            pair(h, put)
            return carry

        lax.fori_loop(at, end, step, 0, unroll=min(2, end - at))

    def chunk_copy(k):
        at, end = chunks[k][0] // 2, chunks[k][1] // 2
        return copy(msend.at[pl.ds(PACK * at, PACK * (end - at))], mbufs[k].at[1], (6, 10, 11)[k], (r, peer(2)))

    patch_copies = [chunk_copy(k) for k in range(3)]
    extract(0, cross, False)

    @pl.when(j_me >= 2)
    def _():
        pl.semaphore_wait(ready.at[2], 1)

    patch_copies[0].start()
    extract(1, cross, False)
    patch_copies[1].start()
    extract(0, mine, True)
    extract(1, mine, True)

    @pl.when(row_low)
    def _():
        up_copy.wait_recv()
        up_mate_copy.wait_recv()
        for f in range(4):
            for i in range(2):
                slab[f, i, pl.ds(base_row, 8), :] = xlow[0, f, i]
                slab[f, i, pl.ds(mate_row, 8), :] = xlow[1, f, i]

    @pl.when(jnp.logical_not(row_low))
    def _():
        for f in range(4):
            for i in range(2):
                slab[f, i] = jnp.zeros((32, 128), F32)

    extract(2, cross, False)
    patch_copies[2].start()
    extract(2, mine, True)

    def coarse_load(f, x, delta=0):
        return slab[f, x, pl.ds(base_row + delta, 8), :]

    def coarse_plane(x, carry):
        fxl, mx, sx, sn, ax = carry
        snn = coarse_load(0, x + 4)
        an = coarse_load(1, x + 3)
        mn = minmod(sn - sx, snn - sn)
        fxu = flux(sx, mx, sn, mn, ax + an)
        ys = [coarse_load(0, x + 2, d) for d in (-2, -1, 0, 1, 2)]
        yb = [coarse_load(2, x + 2, d) for d in (-1, 0, 1)]
        fyl, fyu = y_fluxes(ys, yb)
        vz = coarse_load(3, x + 2)
        up = jnp.where(l127, 0.0, pltpu.roll(sx, 127, 1))
        dn = jnp.where(l0, 0.0, pltpu.roll(sx, 1, 1))
        mz = minmod(sx - dn, up - sx)
        mu = jnp.where(l127, 0.0, pltpu.roll(mz, 127, 1))
        vu = jnp.where(l127, 0.0, pltpu.roll(vz, 127, 1))
        fzu = flux(sx, mz, up, mu, vz + vu)
        w0 = jnp.minimum(vz, 0.0)
        fzl = jnp.where(l0, w0 * (sx - (0.5 + 0.15 * w0) * mz), pltpu.roll(fzu, 1, 1))
        new = sx - 0.3 * ((fxu - fxl) + (fyu - fyl) + (fzu - fzl))
        k = x // 18
        i = x - 18 * k
        mid = jnp.where((i >= 1) & (i <= 16), 1.0, 0.0).astype(F32)
        lowx = jnp.where(i == 0, 0.3, 0.0).astype(F32)
        highx = jnp.where(i == 17, 0.3, 0.0).astype(F32)
        cov = masks[k, 4]
        new = new + mid * (masks[k, 0] * fyu - masks[k, 1] * fyl + masks[k, 2] * fzu - masks[k, 3] * fzl)
        new = new + cov * (lowx * fxu - highx * fxl)
        base[x] = jnp.where(cov * mid > 0, 0.0, new)
        return fxu, mn, sn, snn, an

    def coarse_group(h, carry):
        for e in range(6):
            carry = coarse_plane(6 * h + e, carry)
        return carry

    def coarse_start(x):
        p0, p1, p2, p3 = [coarse_load(0, x + i) for i in range(4)]
        v1, v2 = coarse_load(1, x + 1), coarse_load(1, x + 2)
        m1, m2 = minmod(p1 - p0, p2 - p1), minmod(p2 - p1, p3 - p2)
        return flux(p1, m1, p2, m2, v1 + v2), m2, p2, p3, v2

    lax.fori_loop(0, 5, coarse_group, coarse_start(0))

    @pl.when(turned_dn)
    def _():
        pl.semaphore_wait(ready.at[5], 1)
        down_copy.start()

    my_par = pick(par, j_me)
    my_oy = pick(oyv, j_me)
    my_oz = pick(ozv, j_me)
    sel = jnp.where(my_par // 2 == j_me // 2, zero, one)
    zi = lax.broadcasted_iota(jnp.int32, (128, 512), 0)
    qi = lax.broadcasted_iota(jnp.int32, (128, 512), 1)
    lq = qi & 127
    cell0 = my_oz + (lq >> 1)
    cell1 = jnp.where(lq < 4, my_oz + 64 + (lq >> 1), jnp.where(lq >= 124, my_oz + ((lq - 128) >> 1), -1000))
    cell = jnp.where((qi & 128) == 0, cell0, cell1)
    slope = jnp.where(qi >= 256, jnp.where((qi & 1) == 0, -0.125, 0.125), 0.0)
    zi = jnp.where((zi < 70) & (zi + my_oz >= 3) & (zi + my_oz < 131), zi + my_oz - 3, -5000)
    zmat = jnp.where(zi == cell, 1.0, 0.0) + jnp.where(zi == cell + 1, slope, 0.0) - jnp.where(zi == cell - 1, slope, 0.0)
    zmat = zmat.astype(jnp.bfloat16)

    ri = lax.broadcasted_iota(jnp.int32, (128, 128), 0)
    ci = lax.broadcasted_iota(jnp.int32, (128, 128), 1)
    to_zs[0] = jnp.where(ci == my_oz + (ri >> 1), 1.0, 0.0).astype(jnp.bfloat16)
    to_zface = jnp.where((ri == 127) & (ci == my_oz + 64), 1.0, 0.0) - jnp.where((ri == 0) & (ci == my_oz - 1), 1.0, 0.0)
    to_zs[1] = to_zface.astype(jnp.bfloat16)
    same = (ri >> 3) == (ci >> 3)
    yr, yc = ri & 7, ci & 7
    to_ys[0] = jnp.where(same & (yr == my_oy + (yc >> 1)), 1.0, 0.0).astype(jnp.bfloat16)
    to_yface = jnp.where(same & (yc == 7) & (yr == my_oy + 4), 1.0, 0.0) - jnp.where(same & (yc == 0) & (yr == my_oy - 1), 1.0, 0.0)
    to_ys[1] = to_yface.astype(jnp.bfloat16)

    def unpack_chunk(k):
        at, end = chunks[k]
        patch_copies[k].wait_recv()

        def unpack(h, carry):
            tiles = [mbufs[k][sel, PACK * (h - at // 2) + q] for q in range(PACK)]
            rest = tiles[4]
            for e in range(2):
                first, second = tiles[2 * e], tiles[2 * e + 1]
                to = TILES * (2 * h + e)
                for f, value in enumerate((first, pltpu.roll(first, 64, 1), second, pltpu.roll(second, 64, 1))):
                    wide[to + f] = jnp.where(lane < 64, value, pltpu.roll(rest, (120 - 24 * e - 6 * f) % 128, 1))
                wide[to + 4] = jnp.where(row < 4, pltpu.roll(rest, 6, 0), pltpu.roll(rest, 2, 0)) if e else rest
            return carry

        lax.fori_loop(at // 2, end // 2, unpack, 0, unroll=min(2, (end - at) // 2))
        part, size = pl.ds(TILES * at, TILES * (end - at)), TILES * (end - at)
        res = split_dot(wide[part].reshape(size * 8, 128), zmat)
        for q in range(4):
            gh[q, part] = res[:, 128 * q:128 * (q + 1)].reshape(size, 8, 128)

    def refine_plane(i, full):
        for lt in range(2):
            edge = gh[lt, TILES * i + 4]
            for f in range(4):
                g = gh[lt, TILES * i + f]
                sx = 0.125 * (gh[lt, TILES * (i + 1) + f] - gh[lt, TILES * (i - 1) + f])
                lo = pltpu.roll(g, 1, 0)
                hi = pltpu.roll(g, 7, 0)
                if f == 0:
                    lo = jnp.where(row == 0, edge, lo)
                    hi = jnp.where(row == 7, edge, hi)
                if f == 2:
                    lo = jnp.where(row == 0, pltpu.roll(edge, 7, 0), lo)
                    hi = jnp.where(row == 7, pltpu.roll(edge, 1, 0), hi)
                sy = 0.125 * (hi - lo)
                ctr = gh[2 + lt, TILES * i + f]
                for e in range(2):
                    cx = ctr + sx if e else ctr - sx
                    for ey in range(2):
                        value = cx + sy if ey else cx - sy
                        xf = 2 * (i - 1) + e
                        if full or lt == 1:
                            fine[f, lt, xf, pl.ds(ey, 8, stride=2), :] = value
                        else:
                            fine[f, lt, xf, pl.ds(ey, 2, stride=2), :] = value[0:2]
                            fine[f, lt, xf, pl.ds(12 + ey, 2, stride=2), :] = value[6:8]

    def refine(at, end, full):
        def step(i, carry):
            refine_plane(i, full)
            return carry

        lax.fori_loop(at, end, step, 0)

    def zup(t0, t1):
        a0, a1 = pltpu.roll(t0, 127, 1), pltpu.roll(t1, 127, 1)
        return jnp.where(l127, a1, a0), jnp.where(l127, a0, a1)

    def zdn(t0, t1):
        a0, a1 = pltpu.roll(t0, 1, 1), pltpu.roll(t1, 1, 1)
        return jnp.where(l0, a1, a0), jnp.where(l0, a0, a1)

    def z_fluxes(t0, t1, w0, w1):
        u0, u1 = zup(t0, t1)
        d0, d1 = zdn(t0, t1)
        n0, n1 = minmod(t0 - d0, u0 - t0), minmod(t1 - d1, u1 - t1)
        nu0, nu1 = zup(n0, n1)
        wu0, wu1 = zup(w0, w1)
        h0, h1 = flux(t0, n0, u0, nu0, w0 + wu0), flux(t1, n1, u1, nu1, w1 + wu1)
        b0, b1 = zdn(h0, h1)
        return b0, h0, b1, h1

    def load(block, f, x, d=0):
        if block == 0:
            return fine[f, 0, x, pl.ds(4 + d, 8), :]
        if block == 1:
            return fine[f, 1, x, pl.ds(4 + d, 8), :]
        return jnp.where(row < 4, fine[f, 0, x, pl.ds(2 + d, 8), :], fine[f, 0, x, pl.ds(6 + d, 8), :])

    def load_pad(f, x):
        return jnp.where(row < 4, fine[f, 1, x, pl.ds(2, 8), :], fine[f, 1, x, pl.ds(6, 8), :])

    def x_start(block, x):
        a0, a1, a2, a3 = [load(block, 0, x + d) for d in (-2, -1, 0, 1)]
        w0, w1 = load(block, 1, x - 1), load(block, 1, x)
        n1, n2 = minmod(a1 - a0, a2 - a1), minmod(a2 - a1, a3 - a2)
        return flux(a1, n1, a2, n2, w0 + w1), n2, a2, a3, w1

    def x_next(block, x, carry):
        fxl, mx, sx, sn, ax = carry
        snn = load(block, 0, x + 2)
        an = load(block, 1, x + 1)
        mn = minmod(sn - sx, snn - sn)
        fxu = flux(sx, mx, sn, mn, ax + an)
        return fxl, fxu, (fxu, mn, sn, snn, an)

    def first_plane(x, carries):
        out, xs, ys = [], [], []
        for block in range(3):
            fxl, fxu, nxt = x_next(block, x, carries[block])
            out.append(nxt)
            xs.append((fxl, fxu))
            ys.append(y_fluxes([load(block, 0, x, d) for d in (-2, -1, 0, 1, 2)], [load(block, 2, x, d) for d in (-1, 0, 1)]))
        c0, c1, c2 = carries[0][2], carries[1][2], carries[2][2]
        zl0, zu0, zl1, zu1 = z_fluxes(c0, c1, load(0, 3, x), load(1, 3, x))
        zl2, zu2, _, _ = z_fluxes(c2, load_pad(0, x), load(2, 3, x), load_pad(3, x))
        news = []
        for sc, (xl, xu), (yl, yu), (zl, zu) in zip((c0, c1, c2), xs, ys, ((zl0, zu0), (zl1, zu1), (zl2, zu2))):
            news.append(sc - 0.3 * ((xu - xl) + (yu - yl) + (zu - zl)))
        s1[x - 2, pl.ds(2, 8), :] = news[0]
        s1[x - 2, pl.ds(0, 2), :] = news[2][0:2]
        s1[x - 2, pl.ds(10, 2), :] = news[2][6:8]
        s1z[x - 2] = news[1]
        reg_y = jnp.where(row == 0, ys[0][0], jnp.where(row == 7, ys[0][1], 0.0))
        reg_z = jnp.where(l0, zl0, jnp.where(l127, zu0, 0.0))
        return tuple(out), reg_y, reg_z, xs[0][1]

    def first_pair(h, carries):
        carries, ya, za, _ = first_plane(2 + 2 * h, carries)
        carries, yb, zb, fx = first_plane(3 + 2 * h, carries)
        ry[h] = ya + yb
        rz[h] = za + zb
        fxs[h] = fx
        return carries

    def first_group(h, carries):
        for e in range(2):
            carries = first_pair(2 * h + e, carries)
        return carries

    unpack_chunk(0)
    refine(3, 13, False)
    carries = lax.fori_loop(1, 5, first_group, tuple(x_start(block, 6) for block in range(3)))
    unpack_chunk(1)
    refine(13, 19, False)
    refine(19, 21, True)
    lax.fori_loop(5, 9, first_group, carries)
    unpack_chunk(2)
    refine(1, 3, True)
    first_group(0, tuple(x_start(block, 2) for block in range(3)))

    def second_load(x, d=0):
        return s1[x + 2, pl.ds(2 + d, 8), :]

    def second_plane(x, carry):
        fxl, mx, sx, sn, ax = carry
        snn = second_load(x + 2)
        an = load(0, 1, x + 5)
        mn = minmod(sn - sx, snn - sn)
        fxu = flux(sx, mx, sn, mn, ax + an)
        yl, yu = y_fluxes([second_load(x, d) for d in (-2, -1, 0, 1, 2)], [load(0, 2, x + 4, d) for d in (-1, 0, 1)])
        zl, zu, _, _ = z_fluxes(sx, s1z[x + 2], load(0, 3, x + 4), load(1, 3, x + 4))
        new = sx - 0.3 * ((fxu - fxl) + (yu - yl) + (zu - zl))
        out_f[x] = new
        reg_y = jnp.where(row == 0, yl, jnp.where(row == 7, yu, 0.0))
        reg_z = jnp.where(l0, zl, jnp.where(l127, zu, 0.0))
        return (fxu, mn, sn, snn, an), new, reg_y, reg_z

    def second_pair(h, carry):
        carry, na, ya, za = second_plane(2 * h, carry)
        carry, nb, yb, zb = second_plane(2 * h + 1, carry)
        at = pl.ds(pl.multiple_of(8 * h, 8), 8)
        wavg[0, at, :] = 0.125 * (na + nb)
        wavg[1, at, :] = 0.0375 * (rz[h + 1] + (za + zb))
        wavg[2, at, :] = 0.0375 * (ry[h + 1] + (ya + yb))
        return carry

    q0, q1, q2, q3 = [second_load(i) for i in (-2, -1, 0, 1)]
    u1, u2 = load(0, 1, 3), load(0, 1, 4)
    k1, k2 = minmod(q1 - q0, q2 - q1), minmod(q2 - q1, q3 - q2)
    x_low = flux(q1, k1, q2, k2, u1 + u2)
    def second_group(h, carry):
        for e in range(4):
            carry = second_pair(4 * h + e, carry)
        return carry

    def place(at, count):
        part = pl.ds(8 * at, 8 * count)
        to_y, to_yface = to_ys[0, 0:8 * count, 0:8 * count], to_ys[1, 0:8 * count, 0:8 * count]
        placed = split_dot(wavg[0, part], to_zs[0]) + split_dot(wavg[1, part], to_zs[1])
        faces = split_dot(wavg[2, part], to_zs[0])
        middle = split_dot_left(to_y, placed) + split_dot_left(to_yface, faces)
        vsend[pl.ds(at, count)] = middle.reshape(count, 8, 128)

    @pl.when(j_me == 3)
    def _():
        pl.semaphore_wait(ready.at[3], 1)

    def back_copy(d, k):
        part = pl.ds(8 * k, 8 + 2 * k)
        return copy(vsend.at[part], vrecv.at[d, part], 6 + d if k == 0 else 11 + d, (r, peer(d)))

    back = [[back_copy(d, k) for d in (2, 3, 1)] for k in range(2)]
    carry = lax.fori_loop(0, 2, second_group, (x_low, k2, q2, q3, u2))
    place(0, 8)
    for one_copy in back[0]:
        one_copy.start()
    x_high = lax.fori_loop(2, 4, second_group, carry)[0]
    wx[pl.ds(0, 8), :] = -0.0375 * (fxs[0] + x_low)
    wx[pl.ds(8, 8), :] = 0.0375 * (fxs[16] + x_high)
    place(8, 8)
    vsend[pl.ds(16, 2)] = split_dot_left(to_ys[0, 0:16, 0:16], split_dot(wx[...], to_zs[0])).reshape(2, 8, 128)
    for one_copy in back[1]:
        one_copy.start()
    back = back[0] + back[1]
    vrecv[0] = jnp.zeros((18, 8, 128), F32)

    coarse_carry = lax.fori_loop(5, 10, coarse_group, coarse_start(30))
    for x in (60, 61):
        coarse_carry = coarse_plane(jnp.int32(x), coarse_carry)

    @pl.when(row_high)
    def _():
        down_copy.wait_recv()
        for f in range(2):
            for i in range(2):
                slab[f, NX + 2 + i, pl.ds(base_row, 8), :] = xhigh[f, i]

    @pl.when(jnp.logical_not(row_high))
    def _():
        for f in range(2):
            for i in range(2):
                slab[f, NX + 2 + i] = jnp.zeros((32, 128), F32)

    for x in (62, 63):
        coarse_carry = coarse_plane(jnp.int32(x), coarse_carry)
    for x in range(54, NX):
        out_c[x] = base[x]
    for one_copy in back:
        one_copy.wait_recv()
    for k in range(3):
        def finish(i, carry, k=k):
            out_c[18 * k + 1 + i] = base[18 * k + 1 + i] + vrecv[slots[k], i]
            return carry

        lax.fori_loop(0, 16, finish, 0, unroll=8)
        for x, i in ((18 * k, 16), (18 * k + 17, 17)):
            out_c[x] = base[x] + vrecv[slots[k], i]
    for one_copy in box_copies + patch_copies + back:
        one_copy.wait_send()

    @pl.when(has_side)
    def _():
        near_copy.wait_send()
        hand_copy.wait_send()

    @pl.when(row_low)
    def _():
        down_copy.wait_send()

    @pl.when(row_high)
    def _():
        up_copy.wait_send()
        up_mate_copy.wait_send()


def per_device(*args):
    vmem = pl.BlockSpec(memory_space=pltpu.VMEM)

    def buf(*shape):
        return pltpu.VMEM(shape + (8, 128), F32)

    return pl.pallas_call(
        kernel,
        out_shape=(
            jax.ShapeDtypeStruct((64, 8, 128), F32),
            jax.ShapeDtypeStruct((32, 8, 128), F32),
        ),
        in_specs=[pl.BlockSpec(memory_space=pl.ANY)] * 9,
        out_specs=(vmem, vmem),
        scratch_shapes=[
            buf(3, NX),
            buf(3, NX),
            buf(32),
            buf(3, 32),
            buf(3, 32),
            pltpu.SMEM((1, args[6].shape[1]), jnp.int32),
            pltpu.SMEM((1, args[6].shape[1]), jnp.int32),
            pltpu.SMEM((1, args[6].shape[1]), jnp.int32),
            buf(2, 4, 2),
            buf(2, 2),
            buf(3 * NX // 4),
            buf(2, 3 * NX // 4),
            pltpu.VMEM((4, NX + 4, 32, 128), F32),
            buf(WX // 2 * PACK),
            buf(2, 6 * PACK),
            buf(2, 4 * PACK),
            buf(2, PACK),
            buf(WX * TILES),
            buf(NX),
            buf(4, 5),
            buf(4, WX * TILES),
            pltpu.VMEM((4, 2, 40, 16, 128), F32),
            pltpu.VMEM((36, 16, 128), F32),
            buf(36),
            buf(18),
            buf(18),
            buf(18),
            pltpu.VMEM((3, 128, 128), F32),
            pltpu.VMEM((16, 128), F32),
            pltpu.VMEM((2, 128, 128), jnp.bfloat16),
            pltpu.VMEM((2, 128, 128), jnp.bfloat16),
            buf(18),
            buf(4, 18),
            pltpu.SemaphoreType.DMA((24,)),
            pltpu.SemaphoreType.DMA((16,)),
            pltpu.SemaphoreType.DMA((16,)),
            pltpu.SemaphoreType.REGULAR((6,)),
        ],
        compiler_params=pltpu.CompilerParams(
            collective_id=0, has_side_effects=True, vmem_limit_bytes=60 * 1024 * 1024
        ),
    )(*args)


def solution(mesh):
    in_specs = (
        P("row", "col", None),
        P(None, "row", "col", None),
        P(None, "row", "col", None),
        P("row", "col", None),
        P(None, "row", "col", None),
        P(None, "row", "col", None),
        P("row", None),
        P("row", None),
        P("row", None),
    )
    out_specs = (P("row", "col", None), P("row", "col", None))
    return jax.shard_map(
        per_device, mesh=mesh, in_specs=in_specs, out_specs=out_specs, check_vma=False
    )
```

```python
import jax
import jax.numpy as jnp
from jax import lax
from jax.experimental import pallas as pl
from jax.experimental.pallas import tpu as pltpu
from jax.sharding import PartitionSpec as P

MESH = pl.DeviceIdType.MESH
F32 = jnp.float32
NX = 64
WX = 22
TILES = 5
PACK = 5


def minmod(p, q):
    return jnp.maximum(jnp.minimum(p, q), 0.0) + jnp.minimum(jnp.maximum(p, q), 0.0)


def flux(sl, ml, sr, mr, w):
    q = 0.15 * w
    return w * jnp.where(w > 0, sl + (0.5 - q) * ml, sr - (0.5 + q) * mr)


def split_dot(values, matrix):
    high = values.astype(jnp.bfloat16)
    low = (values - high.astype(F32)).astype(jnp.bfloat16)
    return jnp.dot(high, matrix, preferred_element_type=F32) + jnp.dot(low, matrix, preferred_element_type=F32)


def split_dot_left(matrix, values):
    high = values.astype(jnp.bfloat16)
    low = (values - high.astype(F32)).astype(jnp.bfloat16)
    return jnp.dot(matrix, high, preferred_element_type=F32) + jnp.dot(matrix, low, preferred_element_type=F32)


def tile_iota(dim):
    return lax.broadcasted_iota(jnp.int32, (8, 128), dim)


def y_fluxes(s, b):
    d = [s[i + 1] - s[i] for i in range(4)]
    m = [minmod(d[i], d[i + 1]) for i in range(3)]
    low = flux(s[1], m[0], s[2], m[1], b[0] + b[1])
    high = flux(s[2], m[1], s[3], m[2], b[1] + b[2])
    return low, high


def kernel(
    cs_h, cv_h, cp_h, fs_h, fv_h, fp_h, shift_h, offy_h, offz_h,
    out_c, out_f,
    cv, cp, fs, fv, fp, shift, offy, offz,
    xlow, xhigh, ysend, yrecv, slab, msend, mbuf0, mbuf1, mbuf2, wide, base, masks,
    gh, fine, s1, s1z, fxs, ry, rz, wavg, wx, to_zs, to_ys, vsend, vrecv,
    load_sem, send_sem, recv_sem, ready,
):
    rows = lax.axis_size("row")
    cols = lax.axis_size("col")
    r = lax.axis_index("row")
    c = lax.axis_index("col")
    core = lax.rem(c, 2)
    j_me = lax.rem(c, 4)
    g0 = c - j_me
    sgn = 2 * core - 1
    mate = c + 1 - 2 * core
    chip = c // 2
    has_low = chip > 0
    has_high = chip < cols // 2 - 1
    row_low = r > 0
    row_high = r < rows - 1
    has_side = jnp.where(core == 0, has_low, has_high)

    base_row = pl.multiple_of(8 + 8 * core, 8)
    mate_row = pl.multiple_of(16 - 8 * core, 8)
    my_rows = pl.ds(base_row, 8)
    mate_rows = pl.ds(mate_row, 8)
    half = NX // 2
    pairs = [(shift_h, shift), (offy_h, offy), (offz_h, offz)]
    for h in range(2):
        xs = pl.ds(half * h, half)
        pairs.append((cs_h.at[xs], slab.at[0, pl.ds(2 + half * h, half), my_rows]))
        pairs += [(cv_h.at[f, xs], cv.at[f, xs]) for f in range(3)] + [(cp_h.at[f, xs], cp.at[f, xs]) for f in range(3)]
    pairs += [(fs_h, fs)] + [(fv_h.at[f], fv.at[f]) for f in range(3)] + [(fp_h.at[f], fp.at[f]) for f in range(3)]
    loads = [pltpu.make_async_copy(src, dst, load_sem.at[k]) for k, (src, dst) in enumerate(pairs)]
    for load_copy in loads:
        load_copy.start()

    def peer(d):
        bit0, bit1 = lax.rem(j_me, 2), j_me // 2
        if d & 1:
            bit0 = 1 - bit0
        if d & 2:
            bit1 = 1 - bit1
        return g0 + 2 * bit1 + bit0

    near = c + sgn

    barrier = pltpu.get_barrier_semaphore()

    def greet(*dev):
        pl.semaphore_signal(barrier, inc=1, device_id=dev, device_id_type=MESH)

    above = {1: core == 0, 2: j_me < 2, 3: j_me < 2}
    turned_up = (r == 0) & (c < 4)
    turned_dn = (r == 1) & (c < 4)

    for d in (1, 2, 3):
        @pl.when(jnp.logical_not(above[d]))
        def _(d=d):
            greet(r, peer(d))

    @pl.when((j_me == 0) & has_low)
    def _():
        greet(r, c - 1)

    @pl.when(row_high & jnp.logical_not(turned_up))
    def _():
        greet(r + 1, c)
        greet(r + 1, mate)

    @pl.when(turned_dn)
    def _():
        greet(r - 1, c)
        greet(r - 1, mate)

    greeters = 3 - j_me + jnp.where(has_high & (j_me == 3), 1, 0)
    greeters = greeters + jnp.where(row_low & jnp.logical_not(turned_dn), 2, 0) + jnp.where(turned_up & row_high, 2, 0)

    @pl.when(greeters > 0)
    def _():
        pl.semaphore_wait(barrier, greeters)

    def answer(k, *dev):
        pl.semaphore_signal(ready.at[k], inc=1, device_id=dev, device_id_type=MESH)

    for d in (1, 2, 3):
        @pl.when(above[d])
        def _(d=d):
            answer(d, r, peer(d))

    @pl.when((j_me == 3) & has_high)
    def _():
        answer(4, r, c + 1)

    @pl.when(row_low & jnp.logical_not(turned_dn))
    def _():
        answer(0, r - 1, c)
        answer(0, r - 1, mate)

    @pl.when(turned_up & row_high)
    def _():
        answer(5, r + 1, c)

    row = tile_iota(0)
    lane = tile_iota(1)
    l0 = lane == 0
    l127 = lane == 127

    for k in range(3):
        loads[k].wait()
    par = [j + shift[0, g0 + j] for j in range(4)]
    oyv = [offy[0, g0 + j] for j in range(4)]
    ozv = [offz[0, g0 + j] for j in range(4)]
    one = jnp.int32(1)
    zero = jnp.int32(0)
    rank = []
    for j in range(4):
        acc = zero
        for i in range(j):
            acc = acc + jnp.where(par[i] == par[j], one, zero)
        rank.append(acc)

    def pick(values, t):
        acc = zero
        for j in range(4):
            acc = acc + jnp.where(t == j, values[j], zero)
        return acc

    def half_plane(x):
        values = [0.75 * cv[f, x] - 0.25 * cp[f, x] for f in range(3)]
        for f in range(3):
            slab[f + 1, x + 2, my_rows, :] = values[f]
        return [slab[0, x + 2, my_rows, :]] + values

    def rows_at(value, at):
        return jnp.where(core == 0, pltpu.roll(value, at, 0) if at else value, pltpu.roll(value, (at + 2) % 8, 0))

    def half_coarse(h, carry):
        planes = [half_plane(4 * h + e) for e in range(4)]
        for t in range(2):
            tile = rows_at(planes[2 * t][0], 0)
            for k, value in ((2, planes[2 * t][2]), (4, planes[2 * t + 1][0]), (6, planes[2 * t + 1][2])):
                tile = jnp.where(row >= k, rows_at(value, k), tile)
            ysend[3 * h + t] = tile
        tile = None
        for e in range(4):
            for q in range(2):
                value, at = planes[e][2 * q + 1], 2 * e + q
                moved = jnp.where(core == 0, pltpu.roll(value, at, 0) if at else value, pltpu.roll(value, (at + 1) % 8, 0))
                tile = moved if tile is None else jnp.where(row >= at, moved, tile)
        ysend[3 * h + 2] = tile
        return carry

    def copy(src, dst, k, dev, kr=None):
        return pltpu.make_async_remote_copy(
            src_ref=src, dst_ref=dst, send_sem=send_sem.at[k], recv_sem=recv_sem.at[k if kr is None else kr],
            device_id=dev, device_id_type=MESH,
        )

    boxes = [slab.at[:, pl.ds(2 + half * h, half), my_rows] for h in range(2)]
    box_copies = [copy(boxes[h], boxes[h], 15 * h, (r, mate)) for h in range(2)]
    for k in range(3, 10):
        loads[k].wait()
    lax.fori_loop(0, NX // 8, half_coarse, 0)

    @pl.when(core == 0)
    def _():
        box_copies[0].start()

    for k in range(10, 17):
        loads[k].wait()
    lax.fori_loop(NX // 8, NX // 4, half_coarse, 0)

    up_copy = copy(slab.at[:, pl.ds(NX, 2), my_rows], xlow.at[0], 1, (r + 1, c))
    up_mate_copy = copy(slab.at[:, pl.ds(NX, 2), my_rows], xlow.at[1], 2, (r + 1, mate))
    down_copy = copy(slab.at[pl.ds(0, 2), pl.ds(2, 2), my_rows], xhigh, 3, (r - 1, c))
    near_copy = copy(ysend, yrecv.at[1 - core], 4, (r, near), 5 - core)
    hand_copy = copy(yrecv.at[core], yrecv.at[core], 5, (r, mate), 4 + core)

    @pl.when((core == 1) & has_high)
    def _():
        near_copy.start()

    @pl.when(core == 1)
    def _():
        pl.semaphore_wait(ready.at[1], 1)
        box_copies[0].start()

    box_copies[1].start()

    @pl.when((j_me == 0) & has_low)
    def _():
        pl.semaphore_wait(ready.at[4], 1)
        near_copy.start()

    @pl.when(j_me == 2)
    def _():
        pl.semaphore_wait(ready.at[3], 1)
        near_copy.start()

    @pl.when(turned_up & row_high)
    def _():
        up_copy.start()
        up_mate_copy.start()

    @pl.when(row_low & jnp.logical_not(turned_dn))
    def _():
        down_copy.start()

    def half_fine(x, carry):
        fine[0, 0, x + 4, pl.ds(4, 8), :] = fs[x]
        for f in range(3):
            fine[f + 1, 0, x + 4, pl.ds(4, 8), :] = 0.75 * fv[f, x] - 0.25 * fp[f, x]
        return carry

    for k in range(17, 24):
        loads[k].wait()
    lax.fori_loop(0, 32, half_fine, 0, unroll=4)

    slots = []
    for k in range(3):
        slot, oyk, ozk, valid = zero, zero, zero, zero
        for j in range(4):
            mine = jnp.where((par[j] == j_me) & (rank[j] == k), one, zero)
            dist0 = jnp.where(lax.rem(j_me, 2) == j % 2, zero, one)
            dist1 = jnp.where(j_me // 2 == j // 2, zero, one)
            slot = slot + mine * (dist0 + 2 * dist1)
            oyk = oyk + mine * oyv[j]
            ozk = ozk + mine * ozv[j]
            valid = valid + mine
        slots.append(slot)
        oyk = jnp.where(valid > 0, oyk, -100)
        iny = (row >= oyk) & (row < oyk + 4)
        inz = (lane >= ozk) & (lane < ozk + 64)
        masks[k, 0] = jnp.where((row == oyk - 1) & inz, 0.3, 0.0)
        masks[k, 1] = jnp.where((row == oyk + 4) & inz, 0.3, 0.0)
        masks[k, 2] = jnp.where((lane == ozk - 1) & iny, 0.3, 0.0)
        masks[k, 3] = jnp.where((lane == ozk + 64) & iny, 0.3, 0.0)
        masks[k, 4] = jnp.where(iny & inz, 1.0, 0.0)
    for q in range(5):
        masks[3, q] = jnp.zeros((8, 128), F32)


    @pl.when(has_side)
    def _():
        copy(ysend, yrecv.at[core], 4, (r, near), 4 + core).wait_recv()
        hand_copy.start()

    @pl.when(jnp.where(core == 0, has_high, has_low))
    def _():
        copy(yrecv.at[1 - core], yrecv.at[1 - core], 5, (r, mate), 5 - core).wait_recv()

    for side, has in ((0, has_low), (1, has_high)):
        @pl.when(jnp.logical_not(has))
        def _(side=side):
            yrecv[side] = jnp.zeros((3 * NX // 4, 8, 128), F32)

    @pl.when(row_high & jnp.logical_not(turned_up))
    def _():
        pl.semaphore_wait(ready.at[0], 2)
        up_copy.start()
        up_mate_copy.start()

    def assemble(h, carry):
        for e in range(4):
            x = 4 * h + e
            for side, at in ((0, 6), (1, 24)):
                pair = 3 * h + e // 2
                slab[0, x + 2, pl.ds(at, 2), :] = yrecv[side, pair, pl.ds(4 * (e % 2), 2), :]
                slab[2, x + 2, pl.ds(at, 2), :] = yrecv[side, pair, pl.ds(4 * (e % 2) + 2, 2), :]
                alone = 7 if side == 0 else 24
                slab[1, x + 2, pl.ds(alone, 1), :] = yrecv[side, 3 * h + 2, pl.ds(2 * e, 1), :]
                slab[3, x + 2, pl.ds(alone, 1), :] = yrecv[side, 3 * h + 2, pl.ds(2 * e + 1, 1), :]
        return carry

    lax.fori_loop(0, NX // 4, assemble, 0)
    for one_copy in box_copies:
        one_copy.wait_recv()

    def extractor(t):
        p = pick(par, t)
        first = 18 * pick(rank, t)
        r0 = 5 + 8 * lax.rem(p, 2) + pick(oyv, t)
        turn = 131 - pick(ozv, t)

        def pair(h, put):
            def rolled(value, to):
                return pltpu.roll(value, lax.rem(turn + to, 128), 1)

            rest = []
            for e in range(2):
                x = first + 2 * h + e
                four = [slab[f, x, pl.ds(r0 + 1, 8), :] for f in range(4)]
                edge = slab[0, x, pl.ds(r0, 8), :]
                edge = jnp.where(row == 7, slab[0, x, pl.ds(r0 + 2, 8), :], edge)
                edge = jnp.where(row == 1, slab[2, x, pl.ds(r0 - 1, 8), :], edge)
                edge = jnp.where(row == 6, slab[2, x, pl.ds(r0 + 3, 8), :], edge)
                rest.append((rolled(edge, 0), four))
                put(2 * e, jnp.where(lane < 64, rolled(four[0], 0), rolled(four[1], 64)))
                put(2 * e + 1, jnp.where(lane < 64, rolled(four[2], 0), rolled(four[3], 64)))
            both = jnp.where((row < 2) | (row >= 6), rest[0][0], jnp.where(row < 4, pltpu.roll(rest[1][0], 2, 0), pltpu.roll(rest[1][0], 6, 0)))
            for e in range(2):
                for f in range(4):
                    at = 72 + 24 * e + 6 * f
                    both = jnp.where(lane >= at, rolled(rest[e][1][f], at - 64), both)
            put(4, both)

        return pair

    cross = extractor(lax.rem(j_me + 2, 4))
    mine = extractor(j_me)
    chunks = ((2, 14), (14, WX), (0, 2))
    mbufs = (mbuf0, mbuf1, mbuf2)

    def extract(k, pair, own):
        at, end = chunks[k][0] // 2, chunks[k][1] // 2

        def step(h, carry):
            def put(q, value):
                if own:
                    mbufs[k][0, PACK * (h - at) + q] = value
                else:
                    msend[PACK * h + q] = value

            pair(h, put)
            return carry

        lax.fori_loop(at, end, step, 0, unroll=end - at)

    def chunk_copy(k):
        at, end = chunks[k][0] // 2, chunks[k][1] // 2
        return copy(msend.at[pl.ds(PACK * at, PACK * (end - at))], mbufs[k].at[1], (6, 10, 11)[k], (r, peer(2)))

    patch_copies = [chunk_copy(k) for k in range(3)]
    extract(0, cross, False)

    @pl.when(j_me >= 2)
    def _():
        pl.semaphore_wait(ready.at[2], 1)

    patch_copies[0].start()
    extract(1, cross, False)
    patch_copies[1].start()
    extract(0, mine, True)
    extract(1, mine, True)

    @pl.when(row_low)
    def _():
        up_copy.wait_recv()
        up_mate_copy.wait_recv()
        for f in range(4):
            for i in range(2):
                slab[f, i, pl.ds(base_row, 8), :] = xlow[0, f, i]
                slab[f, i, pl.ds(mate_row, 8), :] = xlow[1, f, i]

    @pl.when(jnp.logical_not(row_low))
    def _():
        for f in range(4):
            for i in range(2):
                slab[f, i] = jnp.zeros((32, 128), F32)

    extract(2, cross, False)
    patch_copies[2].start()
    extract(2, mine, True)

    def coarse_load(f, x, delta=0):
        return slab[f, x, pl.ds(base_row + delta, 8), :]

    def coarse_plane(x, carry):
        fxl, mx, sx, sn, ax = carry
        snn = coarse_load(0, x + 4)
        an = coarse_load(1, x + 3)
        mn = minmod(sn - sx, snn - sn)
        fxu = flux(sx, mx, sn, mn, ax + an)
        ys = [coarse_load(0, x + 2, d) for d in (-2, -1, 0, 1, 2)]
        yb = [coarse_load(2, x + 2, d) for d in (-1, 0, 1)]
        fyl, fyu = y_fluxes(ys, yb)
        vz = coarse_load(3, x + 2)
        up = jnp.where(l127, 0.0, pltpu.roll(sx, 127, 1))
        dn = jnp.where(l0, 0.0, pltpu.roll(sx, 1, 1))
        mz = minmod(sx - dn, up - sx)
        mu = jnp.where(l127, 0.0, pltpu.roll(mz, 127, 1))
        vu = jnp.where(l127, 0.0, pltpu.roll(vz, 127, 1))
        fzu = flux(sx, mz, up, mu, vz + vu)
        w0 = jnp.minimum(vz, 0.0)
        fzl = jnp.where(l0, w0 * (sx - (0.5 + 0.15 * w0) * mz), pltpu.roll(fzu, 1, 1))
        new = sx - 0.3 * ((fxu - fxl) + (fyu - fyl) + (fzu - fzl))
        k = x // 18
        i = x - 18 * k
        mid = jnp.where((i >= 1) & (i <= 16), 1.0, 0.0).astype(F32)
        lowx = jnp.where(i == 0, 0.3, 0.0).astype(F32)
        highx = jnp.where(i == 17, 0.3, 0.0).astype(F32)
        cov = masks[k, 4]
        new = new + mid * (masks[k, 0] * fyu - masks[k, 1] * fyl + masks[k, 2] * fzu - masks[k, 3] * fzl)
        new = new + cov * (lowx * fxu - highx * fxl)
        base[x] = jnp.where(cov * mid > 0, 0.0, new)
        return fxu, mn, sn, snn, an

    def coarse_group(h, carry):
        for e in range(6):
            carry = coarse_plane(6 * h + e, carry)
        return carry

    def coarse_start(x):
        p0, p1, p2, p3 = [coarse_load(0, x + i) for i in range(4)]
        v1, v2 = coarse_load(1, x + 1), coarse_load(1, x + 2)
        m1, m2 = minmod(p1 - p0, p2 - p1), minmod(p2 - p1, p3 - p2)
        return flux(p1, m1, p2, m2, v1 + v2), m2, p2, p3, v2

    lax.fori_loop(0, 5, coarse_group, coarse_start(0))

    @pl.when(turned_dn)
    def _():
        pl.semaphore_wait(ready.at[5], 1)
        down_copy.start()

    my_par = pick(par, j_me)
    my_oy = pick(oyv, j_me)
    my_oz = pick(ozv, j_me)
    sel = jnp.where(my_par // 2 == j_me // 2, zero, one)
    zi = lax.broadcasted_iota(jnp.int32, (128, 512), 0)
    qi = lax.broadcasted_iota(jnp.int32, (128, 512), 1)
    lq = qi & 127
    cell0 = my_oz + (lq >> 1)
    cell1 = jnp.where(lq < 4, my_oz + 64 + (lq >> 1), jnp.where(lq >= 124, my_oz + ((lq - 128) >> 1), -1000))
    cell = jnp.where((qi & 128) == 0, cell0, cell1)
    slope = jnp.where(qi >= 256, jnp.where((qi & 1) == 0, -0.125, 0.125), 0.0)
    zi = jnp.where((zi < 70) & (zi + my_oz >= 3) & (zi + my_oz < 131), zi + my_oz - 3, -5000)
    zmat = jnp.where(zi == cell, 1.0, 0.0) + jnp.where(zi == cell + 1, slope, 0.0) - jnp.where(zi == cell - 1, slope, 0.0)
    zmat = zmat.astype(jnp.bfloat16)

    ri = lax.broadcasted_iota(jnp.int32, (128, 128), 0)
    ci = lax.broadcasted_iota(jnp.int32, (128, 128), 1)
    to_zs[0] = jnp.where(ci == my_oz + (ri >> 1), 1.0, 0.0).astype(jnp.bfloat16)
    to_zface = jnp.where((ri == 127) & (ci == my_oz + 64), 1.0, 0.0) - jnp.where((ri == 0) & (ci == my_oz - 1), 1.0, 0.0)
    to_zs[1] = to_zface.astype(jnp.bfloat16)
    same = (ri >> 3) == (ci >> 3)
    yr, yc = ri & 7, ci & 7
    to_ys[0] = jnp.where(same & (yr == my_oy + (yc >> 1)), 1.0, 0.0).astype(jnp.bfloat16)
    to_yface = jnp.where(same & (yc == 7) & (yr == my_oy + 4), 1.0, 0.0) - jnp.where(same & (yc == 0) & (yr == my_oy - 1), 1.0, 0.0)
    to_ys[1] = to_yface.astype(jnp.bfloat16)

    def unpack_chunk(k):
        at, end = chunks[k]
        patch_copies[k].wait_recv()

        def unpack(h, carry):
            tiles = [mbufs[k][sel, PACK * (h - at // 2) + q] for q in range(PACK)]
            rest = tiles[4]
            for e in range(2):
                first, second = tiles[2 * e], tiles[2 * e + 1]
                to = TILES * (2 * h + e)
                for f, value in enumerate((first, pltpu.roll(first, 64, 1), second, pltpu.roll(second, 64, 1))):
                    wide[to + f] = jnp.where(lane < 64, value, pltpu.roll(rest, (120 - 24 * e - 6 * f) % 128, 1))
                wide[to + 4] = jnp.where(row < 4, pltpu.roll(rest, 6, 0), pltpu.roll(rest, 2, 0)) if e else rest
            return carry

        lax.fori_loop(at // 2, end // 2, unpack, 0, unroll=(end - at) // 2)
        part, size = pl.ds(TILES * at, TILES * (end - at)), TILES * (end - at)
        res = split_dot(wide[part].reshape(size * 8, 128), zmat)
        for q in range(4):
            gh[q, part] = res[:, 128 * q:128 * (q + 1)].reshape(size, 8, 128)

    def refine_plane(i, full):
        for lt in range(2):
            edge = gh[lt, TILES * i + 4]
            for f in range(4):
                g = gh[lt, TILES * i + f]
                sx = 0.125 * (gh[lt, TILES * (i + 1) + f] - gh[lt, TILES * (i - 1) + f])
                lo = pltpu.roll(g, 1, 0)
                hi = pltpu.roll(g, 7, 0)
                if f == 0:
                    lo = jnp.where(row == 0, edge, lo)
                    hi = jnp.where(row == 7, edge, hi)
                if f == 2:
                    lo = jnp.where(row == 0, pltpu.roll(edge, 7, 0), lo)
                    hi = jnp.where(row == 7, pltpu.roll(edge, 1, 0), hi)
                sy = 0.125 * (hi - lo)
                ctr = gh[2 + lt, TILES * i + f]
                for e in range(2):
                    cx = ctr + sx if e else ctr - sx
                    for ey in range(2):
                        value = cx + sy if ey else cx - sy
                        xf = 2 * (i - 1) + e
                        if full or lt == 1:
                            fine[f, lt, xf, pl.ds(ey, 8, stride=2), :] = value
                        else:
                            fine[f, lt, xf, pl.ds(ey, 2, stride=2), :] = value[0:2]
                            fine[f, lt, xf, pl.ds(12 + ey, 2, stride=2), :] = value[6:8]

    def refine(at, end, full):
        def step(i, carry):
            refine_plane(i, full)
            return carry

        lax.fori_loop(at, end, step, 0, unroll=2)

    def zup(t0, t1):
        a0, a1 = pltpu.roll(t0, 127, 1), pltpu.roll(t1, 127, 1)
        return jnp.where(l127, a1, a0), jnp.where(l127, a0, a1)

    def zdn(t0, t1):
        a0, a1 = pltpu.roll(t0, 1, 1), pltpu.roll(t1, 1, 1)
        return jnp.where(l0, a1, a0), jnp.where(l0, a0, a1)

    def z_fluxes(t0, t1, w0, w1):
        u0, u1 = zup(t0, t1)
        d0, d1 = zdn(t0, t1)
        n0, n1 = minmod(t0 - d0, u0 - t0), minmod(t1 - d1, u1 - t1)
        nu0, nu1 = zup(n0, n1)
        wu0, wu1 = zup(w0, w1)
        h0, h1 = flux(t0, n0, u0, nu0, w0 + wu0), flux(t1, n1, u1, nu1, w1 + wu1)
        b0, b1 = zdn(h0, h1)
        return b0, h0, b1, h1

    def load(block, f, x, d=0):
        if block == 0:
            return fine[f, 0, x, pl.ds(4 + d, 8), :]
        if block == 1:
            return fine[f, 1, x, pl.ds(4 + d, 8), :]
        return jnp.where(row < 4, fine[f, 0, x, pl.ds(2 + d, 8), :], fine[f, 0, x, pl.ds(6 + d, 8), :])

    def load_pad(f, x):
        return jnp.where(row < 4, fine[f, 1, x, pl.ds(2, 8), :], fine[f, 1, x, pl.ds(6, 8), :])

    def x_start(block, x):
        a0, a1, a2, a3 = [load(block, 0, x + d) for d in (-2, -1, 0, 1)]
        w0, w1 = load(block, 1, x - 1), load(block, 1, x)
        n1, n2 = minmod(a1 - a0, a2 - a1), minmod(a2 - a1, a3 - a2)
        return flux(a1, n1, a2, n2, w0 + w1), n2, a2, a3, w1

    def x_next(block, x, carry):
        fxl, mx, sx, sn, ax = carry
        snn = load(block, 0, x + 2)
        an = load(block, 1, x + 1)
        mn = minmod(sn - sx, snn - sn)
        fxu = flux(sx, mx, sn, mn, ax + an)
        return fxl, fxu, (fxu, mn, sn, snn, an)

    def first_plane(x, carries):
        out, xs, ys = [], [], []
        for block in range(3):
            fxl, fxu, nxt = x_next(block, x, carries[block])
            out.append(nxt)
            xs.append((fxl, fxu))
            ys.append(y_fluxes([load(block, 0, x, d) for d in (-2, -1, 0, 1, 2)], [load(block, 2, x, d) for d in (-1, 0, 1)]))
        c0, c1, c2 = carries[0][2], carries[1][2], carries[2][2]
        zl0, zu0, zl1, zu1 = z_fluxes(c0, c1, load(0, 3, x), load(1, 3, x))
        zl2, zu2, _, _ = z_fluxes(c2, load_pad(0, x), load(2, 3, x), load_pad(3, x))
        news = []
        for sc, (xl, xu), (yl, yu), (zl, zu) in zip((c0, c1, c2), xs, ys, ((zl0, zu0), (zl1, zu1), (zl2, zu2))):
            news.append(sc - 0.3 * ((xu - xl) + (yu - yl) + (zu - zl)))
        s1[x - 2, pl.ds(2, 8), :] = news[0]
        s1[x - 2, pl.ds(0, 2), :] = news[2][0:2]
        s1[x - 2, pl.ds(10, 2), :] = news[2][6:8]
        s1z[x - 2] = news[1]
        reg_y = jnp.where(row == 0, ys[0][0], jnp.where(row == 7, ys[0][1], 0.0))
        reg_z = jnp.where(l0, zl0, jnp.where(l127, zu0, 0.0))
        return tuple(out), reg_y, reg_z, xs[0][1]

    def first_pair(h, carries):
        carries, ya, za, _ = first_plane(2 + 2 * h, carries)
        carries, yb, zb, fx = first_plane(3 + 2 * h, carries)
        ry[h] = ya + yb
        rz[h] = za + zb
        fxs[h] = fx
        return carries

    def first_group(h, carries):
        for e in range(2):
            carries = first_pair(2 * h + e, carries)
        return carries

    unpack_chunk(0)
    refine(3, 13, False)
    carries = lax.fori_loop(1, 5, first_group, tuple(x_start(block, 6) for block in range(3)), unroll=2)
    unpack_chunk(1)
    refine(13, 19, False)
    refine(19, 21, True)
    lax.fori_loop(5, 9, first_group, carries, unroll=2)
    unpack_chunk(2)
    refine(1, 3, True)
    first_group(0, tuple(x_start(block, 2) for block in range(3)))

    def second_load(x, d=0):
        return s1[x + 2, pl.ds(2 + d, 8), :]

    def second_plane(x, carry):
        fxl, mx, sx, sn, ax = carry
        snn = second_load(x + 2)
        an = load(0, 1, x + 5)
        mn = minmod(sn - sx, snn - sn)
        fxu = flux(sx, mx, sn, mn, ax + an)
        yl, yu = y_fluxes([second_load(x, d) for d in (-2, -1, 0, 1, 2)], [load(0, 2, x + 4, d) for d in (-1, 0, 1)])
        zl, zu, _, _ = z_fluxes(sx, s1z[x + 2], load(0, 3, x + 4), load(1, 3, x + 4))
        new = sx - 0.3 * ((fxu - fxl) + (yu - yl) + (zu - zl))
        out_f[x] = new
        reg_y = jnp.where(row == 0, yl, jnp.where(row == 7, yu, 0.0))
        reg_z = jnp.where(l0, zl, jnp.where(l127, zu, 0.0))
        return (fxu, mn, sn, snn, an), new, reg_y, reg_z

    def second_pair(h, carry):
        carry, na, ya, za = second_plane(2 * h, carry)
        carry, nb, yb, zb = second_plane(2 * h + 1, carry)
        at = pl.ds(pl.multiple_of(8 * h, 8), 8)
        wavg[0, at, :] = 0.125 * (na + nb)
        wavg[1, at, :] = 0.0375 * (rz[h + 1] + (za + zb))
        wavg[2, at, :] = 0.0375 * (ry[h + 1] + (ya + yb))
        return carry

    q0, q1, q2, q3 = [second_load(i) for i in (-2, -1, 0, 1)]
    u1, u2 = load(0, 1, 3), load(0, 1, 4)
    k1, k2 = minmod(q1 - q0, q2 - q1), minmod(q2 - q1, q3 - q2)
    x_low = flux(q1, k1, q2, k2, u1 + u2)
    def second_group(h, carry):
        for e in range(4):
            carry = second_pair(4 * h + e, carry)
        return carry

    def place(at, count):
        part = pl.ds(8 * at, 8 * count)
        to_y, to_yface = to_ys[0, 0:8 * count, 0:8 * count], to_ys[1, 0:8 * count, 0:8 * count]
        placed = split_dot(wavg[0, part], to_zs[0]) + split_dot(wavg[1, part], to_zs[1])
        faces = split_dot(wavg[2, part], to_zs[0])
        middle = split_dot_left(to_y, placed) + split_dot_left(to_yface, faces)
        vsend[pl.ds(at, count)] = middle.reshape(count, 8, 128)

    @pl.when(j_me == 3)
    def _():
        pl.semaphore_wait(ready.at[3], 1)

    def back_copy(d, k):
        part = pl.ds(8 * k, 8 + 2 * k)
        return copy(vsend.at[part], vrecv.at[d, part], 6 + d if k == 0 else 11 + d, (r, peer(d)))

    back = [[back_copy(d, k) for d in (2, 3, 1)] for k in range(2)]
    carry = lax.fori_loop(0, 2, second_group, (x_low, k2, q2, q3, u2))
    place(0, 8)
    for one_copy in back[0]:
        one_copy.start()
    x_high = lax.fori_loop(2, 4, second_group, carry)[0]
    wx[pl.ds(0, 8), :] = -0.0375 * (fxs[0] + x_low)
    wx[pl.ds(8, 8), :] = 0.0375 * (fxs[16] + x_high)
    place(8, 8)
    vsend[pl.ds(16, 2)] = split_dot_left(to_ys[0, 0:16, 0:16], split_dot(wx[...], to_zs[0])).reshape(2, 8, 128)
    for one_copy in back[1]:
        one_copy.start()
    back = back[0] + back[1]
    vrecv[0] = jnp.zeros((18, 8, 128), F32)

    coarse_carry = lax.fori_loop(5, 10, coarse_group, coarse_start(30))
    for x in (60, 61):
        coarse_carry = coarse_plane(jnp.int32(x), coarse_carry)

    @pl.when(row_high)
    def _():
        down_copy.wait_recv()
        for f in range(2):
            for i in range(2):
                slab[f, NX + 2 + i, pl.ds(base_row, 8), :] = xhigh[f, i]

    @pl.when(jnp.logical_not(row_high))
    def _():
        for f in range(2):
            for i in range(2):
                slab[f, NX + 2 + i] = jnp.zeros((32, 128), F32)

    for x in (62, 63):
        coarse_carry = coarse_plane(jnp.int32(x), coarse_carry)
    for x in range(54, NX):
        out_c[x] = base[x]
    for one_copy in back:
        one_copy.wait_recv()
    for k in range(3):
        def finish(i, carry, k=k):
            out_c[18 * k + 1 + i] = base[18 * k + 1 + i] + vrecv[slots[k], i]
            return carry

        lax.fori_loop(0, 16, finish, 0, unroll=8)
        for x, i in ((18 * k, 16), (18 * k + 17, 17)):
            out_c[x] = base[x] + vrecv[slots[k], i]
    for one_copy in box_copies + patch_copies + back:
        one_copy.wait_send()

    @pl.when(has_side)
    def _():
        near_copy.wait_send()
        hand_copy.wait_send()

    @pl.when(row_low)
    def _():
        down_copy.wait_send()

    @pl.when(row_high)
    def _():
        up_copy.wait_send()
        up_mate_copy.wait_send()


def per_device(*args):
    vmem = pl.BlockSpec(memory_space=pltpu.VMEM)

    def buf(*shape):
        return pltpu.VMEM(shape + (8, 128), F32)

    return pl.pallas_call(
        kernel,
        out_shape=(
            jax.ShapeDtypeStruct((64, 8, 128), F32),
            jax.ShapeDtypeStruct((32, 8, 128), F32),
        ),
        in_specs=[pl.BlockSpec(memory_space=pl.ANY)] * 9,
        out_specs=(vmem, vmem),
        scratch_shapes=[
            buf(3, NX),
            buf(3, NX),
            buf(32),
            buf(3, 32),
            buf(3, 32),
            pltpu.SMEM((1, args[6].shape[1]), jnp.int32),
            pltpu.SMEM((1, args[6].shape[1]), jnp.int32),
            pltpu.SMEM((1, args[6].shape[1]), jnp.int32),
            buf(2, 4, 2),
            buf(2, 2),
            buf(3 * NX // 4),
            buf(2, 3 * NX // 4),
            pltpu.VMEM((4, NX + 4, 32, 128), F32),
            buf(WX // 2 * PACK),
            buf(2, 6 * PACK),
            buf(2, 4 * PACK),
            buf(2, PACK),
            buf(WX * TILES),
            buf(NX),
            buf(4, 5),
            buf(4, WX * TILES),
            pltpu.VMEM((4, 2, 40, 16, 128), F32),
            pltpu.VMEM((36, 16, 128), F32),
            buf(36),
            buf(18),
            buf(18),
            buf(18),
            pltpu.VMEM((3, 128, 128), F32),
            pltpu.VMEM((16, 128), F32),
            pltpu.VMEM((2, 128, 128), jnp.bfloat16),
            pltpu.VMEM((2, 128, 128), jnp.bfloat16),
            buf(18),
            buf(4, 18),
            pltpu.SemaphoreType.DMA((24,)),
            pltpu.SemaphoreType.DMA((16,)),
            pltpu.SemaphoreType.DMA((16,)),
            pltpu.SemaphoreType.REGULAR((6,)),
        ],
        compiler_params=pltpu.CompilerParams(
            collective_id=0, has_side_effects=True, vmem_limit_bytes=60 * 1024 * 1024
        ),
    )(*args)


def solution(mesh):
    in_specs = (
        P("row", "col", None),
        P(None, "row", "col", None),
        P(None, "row", "col", None),
        P("row", "col", None),
        P(None, "row", "col", None),
        P(None, "row", "col", None),
        P("row", None),
        P("row", None),
        P("row", None),
    )
    out_specs = (P("row", "col", None), P("row", "col", None))
    return jax.shard_map(
        per_device, mesh=mesh, in_specs=in_specs, out_specs=out_specs, check_vma=False
    )
```
